256 devices in a mesh: rep: 16 (over x_hi, y, core), fsdp: 16 (over x_lo, z).
Axes of the slice: x: 4 (x_hi: 2, x_lo: 2; x = x_hi * 2 + x_lo), y: 4, z: 8, core: 2. Of those that a mesh axis runs over, the one named last changes fastest.
Arguments:
- activations: bfloat16 [65536, 8192], P(('rep', 'fsdp')), may hold values from -0.375 to 0.375
- cotangent: bfloat16 [65536, 512], P(('rep', 'fsdp')), may hold values from -6 to 6
- key_weight: bfloat16 [8192, 512], P('fsdp'), may hold values from -0.25 to 0.25
- momentum: float32 [16, 8192, 512], P('rep', 'fsdp'), may hold values from -6 to 6
- selection: int32 [16, 8192, 256], P('rep', 'fsdp'), may hold values from 0 to 63, as said below
Outputs:
- input_grad: bfloat16 [65536, 8192], P(('rep', 'fsdp'))
- new_momentum: float32 [16, 8192, 512], P('rep', 'fsdp')
- update: float32 [8192, 512], P('fsdp')
The draws below stay inside these ranges and needn't reach their ends.
Inputs may be any that keep to these rules, and one draw needn't show every extreme that they name: `selection`: the 32 entries of one block name 32 different positions of that block of 64 values.
All inputs are finite; a program needn't handle non-finite values.
Results may differ from the reference program's by a relative error of at most 0.0075.
Values may be sent and summed in bfloat16 or wider, within the bound.
A program may use at most 128 MiB of HBM per device.

```python
import jax
import jax.numpy as jnp
from jax import lax

D = 8192
KW = 512
BLOCK = 64
KEEP = 32
TOK_DEV = 256
REPLICAS = 16
TOKENS = 65536
N_FSDP = 16


def draw_selection(key, part):
    key = jax.random.fold_in(key, 5)
    scores = jax.random.randint(key, (REPLICAS, D, KW // BLOCK, BLOCK), 0, 1 << 20)
    scores = scores * BLOCK + jnp.arange(BLOCK, dtype=jnp.int32)
    ranking = jnp.argsort(scores, axis=-1)[..., :KEEP]
    return ranking.reshape(REPLICAS, D, KW // 2).astype(jnp.int32)


def spiked(drawn, own_key, source, target, parts, factor):
    owner, partner = [(jnp.arange(drawn.shape[axis_at]) // (drawn.shape[axis_at] // parts)).reshape([-1 if axis == axis_at else 1 for axis in range(drawn.ndim)]) for axis_at in (source, target)]
    chosen = jax.random.permutation(own_key, parts)[partner]
    strong = (owner == chosen) | (owner == (partner + parts // 2) % parts)
    return jnp.where(strong, factor * drawn, drawn)


def steps_of(key, shape, split, low, top_value):
    level, own = 1.0, jax.random.fold_in(key, 6)
    for position, parts in split:
        draws = jnp.exp(jax.random.uniform(jax.random.fold_in(own, position), (parts,), jnp.float32, low / len(split), top_value / len(split)))
        level = level * jnp.repeat(draws, shape[position] // parts).reshape([-1 if axis == position else 1 for axis in range(len(shape))])
    return level


def centred(stream_key, dims, scale, most, cuts=(), kind=jnp.bfloat16):
    level = steps_of(stream_key, dims, cuts, -0.22, 0.18) if cuts else 1.0
    values = jax.random.normal(stream_key, dims, jnp.float32) * scale * level
    return jnp.minimum(jnp.maximum(values, -most), most).astype(kind)


def gaussian_with(key, shape, spread, reach, shards, heavy, kind=jnp.bfloat16):
    array = spread * jax.random.normal(key, shape, jnp.float32)
    if shards:
        array = array * steps_of(key, shape, shards, -0.22, 0.18)
    return jnp.clip(spiked(array, jax.random.fold_in(key, 3), *heavy), -reach, reach).astype(kind)


def setup_inputs(seed: int = 0) -> dict:
    arg_keys = jax.random.split(jax.random.key(seed), 6)
    activations = gaussian_with(arg_keys[0], (TOKENS, D), ((TOK_DEV * N_FSDP) ** -0.5), 0.375, ((0, 256),), (0, 1, 256, 6.0))
    cotangent = centred(arg_keys[1], (TOKENS, KW), 1.0, 6.0, ((0, 256),))
    key_weight = centred(arg_keys[2], (D, KW), KW ** -0.5, 0.25, ((0, 16),))
    momentum = centred(arg_keys[3], (REPLICAS, D, KW), 1.0, 6.0, ((0, 16), (1, 16)), jnp.float32)
    selection = draw_selection(jax.random.fold_in(arg_keys[5], 71), 0)
    return {"activations": activations, "cotangent": cotangent, "key_weight": key_weight, "momentum": momentum, "selection": selection}


decay_rate = 0.9

def cosine_table(columns):
    row_index = jnp.arange(columns, dtype=jnp.int32)[:, None]
    col_index = jnp.arange(columns, dtype=jnp.int32)[None, :]
    freq = (row_index % BLOCK).astype(jnp.float32)
    where_at = (col_index % BLOCK).astype(jnp.float32)
    base = jnp.sqrt(2.0 / BLOCK) * jnp.cos(jnp.pi * (2.0 * where_at + 1.0) * freq / (2.0 * BLOCK))
    base = jnp.where(row_index % BLOCK == 0, base * jnp.sqrt(0.5), base)
    return jnp.where(row_index // BLOCK == col_index // BLOCK, base, jnp.zeros_like(base))

def chosen_mask(selection, columns):
    row_count = selection.shape[0]
    groups = selection.reshape(row_count, columns // BLOCK, KEEP)
    hits = groups[..., None] == jnp.arange(BLOCK, dtype=jnp.int32)
    return jnp.any(hits, axis=2).reshape(row_count, columns)

def reference(activations, cotangent, key_weight, momentum, selection):
    input_grad = jnp.dot(cotangent, key_weight.T, preferred_element_type=jnp.float32).astype(jnp.bfloat16)
    cosines = cosine_table(KW)
    grouped_x = activations.reshape(REPLICAS, N_FSDP, TOK_DEV, D)
    grouped_c = cotangent.reshape(REPLICAS, N_FSDP, TOK_DEV, KW)

    def replica_step(inputs):
        x_groups, c_groups, moment, picked = inputs

        def accumulate(carry, pair):
            term = jnp.dot(pair[0].T, pair[1], preferred_element_type=jnp.float32)
            return (carry + term.astype(jnp.float32), None)
        gradient = lax.scan(accumulate, jnp.zeros((D, KW), jnp.float32), (x_groups, c_groups))[0]
        blended = decay_rate * moment + gradient
        spectrum = jnp.dot(blended, cosines.T, precision=lax.Precision.HIGHEST)
        chosen = chosen_mask(picked, KW)
        retained = jnp.where(chosen, spectrum, jnp.zeros_like(spectrum))
        renewed = blended - jnp.dot(retained, cosines, precision=lax.Precision.HIGHEST)
        return (renewed, retained.astype(jnp.bfloat16))
    new_momentum, outgoing = lax.map(replica_step, (grouped_x, grouped_c, momentum, selection))
    summed = lax.optimization_barrier(jnp.sum(outgoing.astype(jnp.float32), axis=0))
    update = jnp.dot(summed, cosines, precision=lax.Precision.HIGHEST) / REPLICAS
    return (input_grad, new_momentum, update)
```

```python
import functools

import jax
import jax.numpy as jnp
import ml_dtypes
import numpy as np
from jax import lax
from jax.experimental import pallas as pl
from jax.experimental.pallas import tpu as pltpu
from jax.sharding import PartitionSpec as P

BLOCK = 64
KEEP = 32
DECAY = 0.9
MESH = pl.DeviceIdType.MESH
TOK = 256
D = 8192
KW = 512
SUB = 128
TILE = 256
ROUNDS = 2
RROWS = KW // ROUNDS
PIECE = RROWS // 8
f32, bf16 = jnp.float32, jnp.bfloat16


def cosine_tile():
    k = np.arange(BLOCK)[:, None].astype(np.float64)
    n = np.arange(BLOCK)[None, :].astype(np.float64)
    base = np.sqrt(2.0 / BLOCK) * np.cos(np.pi * (2.0 * n + 1.0) * k / (2.0 * BLOCK))
    base[0] *= np.sqrt(0.5)
    return np.kron(np.eye(TILE // BLOCK), base).astype(np.float32)


def split_np(a):
    hi = a.astype(ml_dtypes.bfloat16)
    lo = (a - hi.astype(np.float32)).astype(ml_dtypes.bfloat16)
    return np.stack([hi, lo])


def split(a):
    hi = a.astype(bf16)
    return hi, (a - hi.astype(f32)).astype(bf16)


def dot(a, b):
    return jnp.dot(a, b, preferred_element_type=f32)


def transform(a, table):
    hi, lo = split(a)
    t_hi, t_lo = table[0], table[1]
    parts = []
    for j in range(a.shape[1] // TILE):
        cols = slice(j * TILE, (j + 1) * TILE)
        parts.append(dot(hi[:, cols], t_hi) + (dot(lo[:, cols], t_hi) + dot(hi[:, cols], t_lo)))
    return parts[0] if len(parts) == 1 else jnp.concatenate(parts, axis=1)


def message(i):
    if i >= 28:
        return 0, i - 28
    sign, half = (1, 0) if i % 2 == 0 else (-1, 2)
    if i < 4:
        return 4, i // 2 + half
    stage, slot = (i - 4) // 8, ((i - 4) % 8) // 2
    if stage == 0 and sign > 0:
        slot = (slot + 2) % 4
    return sign * (3 - stage), slot


def kernel(
    x_ref, c_ref, w_ref, m_ref, s_ref, fwd_ref, inv_ref,
    ig_ref, nm_ref, u_ref,
    xb, cb, zs, zr, wg, igv, mv, sv, mk, out, nmv, uv, cx, pr, rb,
    x_ss, x_rs, x_ls, z_ss, z_rs, wa_ss, wa_rs, wb_ss, wb_rs, wc_ss, wc_rs,
    p_ss, p_rs, g_ss, g_rs, h_ss, h_rs, q_ss, q_rs, l_s, o_s,
):
    r, f = lax.axis_index("rep"), lax.axis_index("fsdp")
    xh, y, c, xl, z = r // 8, (r // 2) % 4, r % 2, f // 8, f % 8
    chip = xh * 4 + y
    piece = y * 2 + c

    def dev(xh=xh, y=y, c=c, xl=xl, z=z):
        return (xh * 8 + (y % 4) * 2 + c, xl * 8 + z % 8)

    x_mate = dev(xl=1 - xl)
    x_other = dev(xh=1 - xh, xl=1 - xl)
    core_mate = dev(c=1 - c)
    z_to = (dev(z=z + 1), dev(z=z + 7))
    chips = [dev(xh=(xh + k // 4) % 2, y=y + k % 4) for k in range(8)]
    peers = [x_mate, x_other, core_mate] + [dev(z=z + k) for k in range(1, 8)] + chips[1:]

    def send(src, dst, ss, rs, to):
        return pltpu.make_async_remote_copy(
            src_ref=src, dst_ref=dst, send_sem=ss, recv_sem=rs, device_id=to, device_id_type=MESH
        )

    barrier = pltpu.get_barrier_semaphore()
    for peer in peers:
        pl.semaphore_signal(barrier, inc=1, device_id=peer, device_id_type=MESH)
    pl.semaphore_wait(barrier, len(peers))

    c_send = send(c_ref, cb.at[pl.ds(TOK, TOK)], x_ss.at[32], x_rs.at[32], x_mate)
    c_send.start()

    def column(half, i):
        away, sub = message(i)
        return pl.multiple_of(half * (D // 2) + ((z + away + 8) % 8) * KW + sub * SUB, SUB)

    def x_send(i):
        return send(
            x_ref.at[:, pl.ds(column(1 - xl, i), SUB)], xb.at[i, pl.ds(TOK, TOK)], x_ss.at[i], x_rs.at[i], x_mate
        )

    def x_load(i):
        return pltpu.make_async_copy(
            x_ref.at[:, pl.ds(column(xl, i), SUB)], xb.at[i, pl.ds(0, TOK)], x_ls.at[i]
        )

    w_src = w_ref.at[pl.ds(pl.multiple_of(piece * 64, 64), 64)]
    wa = [
        send(w_src, wg.at[xl, z, piece], wa_ss.at[k - 1], wa_rs.at[k - 1], dev(z=z + k)) for k in range(1, 8)
    ]
    w_own = pltpu.make_async_copy(w_src, wg.at[xl, z, piece], l_s.at[0])
    c_own = pltpu.make_async_copy(c_ref, cb.at[pl.ds(0, TOK)], l_s.at[1])
    s_own = pltpu.make_async_copy(s_ref.at[0], sv, l_s.at[2])
    m_own = pltpu.make_async_copy(m_ref.at[0], mv, l_s.at[3])

    for i in range(4):
        x_send(i).start()
    for k in (0, 6, 1, 5, 2, 4, 3):
        wa[k].start()
    for i in range(4, 32):
        x_send(i).start()
    s_own.start()
    m_own.start()
    c_own.start()
    w_own.start()
    for i in range(32):
        x_load(i).start()

    s_own.wait()
    sel_row = lax.broadcasted_iota(jnp.int32, (KW // 2, KW), 0) // KEEP
    sel_col = lax.broadcasted_iota(jnp.int32, (KW // 2, KW), 1)
    spread = [
        jnp.where((sel_row == sel_col // BLOCK) & ((sel_col % BLOCK) // 16 == g), 1.0, 0.0).astype(bf16)
        for g in range(4)
    ]
    bit = lax.broadcasted_iota(jnp.int32, (SUB, KW), 1) % 16

    def mask_rows(b, carry):
        rows = pl.ds(pl.multiple_of(b * SUB, SUB), SUB)
        sel = sv[rows, :]
        power = jnp.left_shift(1, sel % 16).astype(f32)
        total = jnp.zeros((SUB, KW), f32)
        for g in range(4):
            total += dot(jnp.where(sel // 16 == g, power, 0.0).astype(bf16), spread[g])
        mk[rows, :] = (jnp.right_shift(total.astype(jnp.int32), bit) % 2).astype(f32)
        return carry

    lax.fori_loop(0, KW // SUB, mask_rows, 0)
    m_own.wait()
    c_own.wait()
    w_own.wait()

    def product(i):
        pltpu.make_async_copy(x_ref.at[:, pl.ds(0, SUB)], xb.at[i, pl.ds(0, TOK)], x_ls.at[i]).wait()
        send(xb.at[i, pl.ds(0, TOK)], xb.at[i, pl.ds(TOK, TOK)], x_ss.at[i], x_rs.at[i], x_mate).wait_recv()
        return lax.dot_general(xb[i], cb[...], (((0,), (0,)), ((), ())), preferred_element_type=f32)

    def z_copy(way, m):
        return send(zs.at[way, m], zr.at[way, m], z_ss.at[way, m], z_rs.at[way, m], z_to[way])

    def step(way, m, i, before):
        total = product(i)
        if before is not None:
            z_copy(way, before).wait_recv()
            total += zr[way, before].astype(f32)
        zs[way, m] = total.astype(bf16)
        z_copy(way, m).start()

    def steps(start, count, first, before):
        def body(k, carry):
            for way in range(2):
                step(way, first + k, start + 2 * k + way, None if before is None else before(way, k))
            return carry

        lax.fori_loop(0, count, body, 0)

    def group(x_side, y_side, core):
        return wg.at[x_side, :, (y_side % 4) * 2 + core]

    wb = [
        send(group(xl, y, c), group(xl, y, c), wb_ss.at[0], wb_rs.at[0], dev(y=y + 1)),
        send(group(xl, y, c), group(xl, y, c), wb_ss.at[1], wb_rs.at[1], dev(y=y + 3)),
        send(group(xl, y, c), group(xl, y, c), wb_ss.at[2], wb_rs.at[2], dev(y=y + 2)),
        send(group(xl, y, c), group(xl, y, c), wb_ss.at[3], wb_rs.at[3], x_other),
        send(group(xl, y + 3, c), group(xl, y + 3, c), wb_ss.at[4], wb_rs.at[4], x_other),
        send(group(1 - xl, y, c), group(1 - xl, y, c), wb_ss.at[5], wb_rs.at[5], dev(y=y + 3)),
        send(group(1 - xl, y + 3, c), group(1 - xl, y + 3, c), wb_ss.at[6], wb_rs.at[6], dev(y=y + 1)),
    ]
    groups = [(xl, y), (xl, y + 3), (xl, y + 1), (xl, y + 2), (1 - xl, y), (1 - xl, y + 3), (1 - xl, y + 1), (1 - xl, y + 2)]
    wc = [
        send(group(*g, c), group(*g, c), wc_ss.at[k], wc_rs.at[k], core_mate) for k, g in enumerate(groups)
    ]

    def input_grad(k):
        half, place = groups[k]
        place = place % 4
        wc[k].wait_recv()

        def body(zz, carry):
            rows = wg[half, zz, pl.ds(place * 2, 2)].reshape(SUB, KW)
            col = pl.multiple_of(half * (D // 2) + zz * KW + place * SUB, SUB)
            igv[:, pl.ds(col, SUB)] = lax.dot_general(
                cb[0:TOK], rows, (((1,), (1,)), ((), ())), preferred_element_type=f32
            ).astype(bf16)
            return carry

        lax.fori_loop(0, 8, body, 0)

    c_send.wait_recv()
    steps(0, 2, 0, None)
    for k in range(7):
        wa[k].wait_recv()
    for k in (3, 0, 1, 2):
        wb[k].start()
    wc[0].start()
    steps(4, 2, 2, None)
    steps(8, 2, 4, lambda way, k: k)
    input_grad(0)
    def at_two(way, k):
        return 2 + ((k + 2) % 4 if way == 0 else k)

    steps(12, 4, 6, at_two)
    wb[0].wait_recv()
    wb[3].wait_recv()
    wb[4].start()
    wb[5].start()
    wc[1].start()
    wc[4].start()
    wb[1].wait_recv()
    wc[2].start()
    input_grad(1)
    input_grad(4)
    input_grad(2)
    steps(20, 4, 10, lambda way, k: 6 + k)
    wb[4].wait_recv()
    wb[6].start()
    wb[2].wait_recv()
    wc[3].start()
    wc[5].start()

    def finish(b):
        rows = pl.ds(b * SUB, SUB)
        total = product(28 + b)
        z_copy(0, 10 + b).wait_recv()
        z_copy(1, 10 + b).wait_recv()
        total += zr[0, 10 + b].astype(f32) + zr[1, 10 + b].astype(f32)
        blended = DECAY * mv[rows, :] + total
        retained = mk[rows, :] * transform(blended, fwd_ref)
        out[rows, :] = retained.astype(bf16)
        nmv[rows, :] = blended - transform(retained, inv_ref)

    mine = pl.ds(pl.multiple_of(c * TILE, TILE), TILE)
    theirs = pl.ds(pl.multiple_of((1 - c) * TILE, TILE), TILE)

    def span(q):
        return pl.ds(q * RROWS, RROWS)

    def pair_copy(q):
        return send(out.at[span(q), theirs], cx.at[q], p_ss.at[q], p_rs.at[q], core_mate)

    def pieces(q, k):
        to = ((xh + k // 4) % 2) * 4 + (y + k) % 4
        return send(pr.at[q, to], rb.at[q, chip], g_ss.at[q, k - 1], g_rs.at[q, k - 1], chips[k])

    own_piece = [pl.ds(pl.multiple_of(q * RROWS + chip * PIECE, PIECE), PIECE) for q in range(ROUNDS)]

    def shares(q, k):
        at = uv.at[own_piece[q], mine]
        return send(at, at, h_ss.at[q, k - 1], h_rs.at[q, k - 1], chips[k])

    def halves(q):
        at = uv.at[span(q), mine]
        return send(at, at, q_ss.at[q], q_rs.at[q], core_mate)

    def scatter(q):
        pair_copy(q).wait_recv()
        both = out[span(q), mine].astype(f32) + cx[q].astype(f32)
        pr[q] = both.astype(bf16).reshape(8, PIECE, TILE)
        for k in range(1, 8):
            pieces(q, k).start()
        rb[q, chip] = pr[q, chip]

    def gather(q):
        for k in range(1, 8):
            pieces(q, k).wait_recv()
        summed = jnp.sum(rb[q].astype(f32), axis=0)
        uv[own_piece[q], mine] = transform(summed, inv_ref) * (1.0 / 16.0)
        for k in range(1, 8):
            shares(q, k).start()

    def exchange(q):
        for k in range(1, 8):
            shares(q, k).wait_recv()
        halves(q).start()

    u_out = [pltpu.make_async_copy(uv.at[span(q)], u_ref.at[span(q)], o_s.at[q]) for q in range(ROUNDS)]
    nm_out = pltpu.make_async_copy(nmv, nm_ref.at[0], o_s.at[ROUNDS])
    ig_out = pltpu.make_async_copy(igv, ig_ref, o_s.at[ROUNDS + 1])

    finish(0)
    finish(1)
    pair_copy(0).start()
    finish(2)
    scatter(0)
    finish(3)
    pair_copy(1).start()
    nm_out.start()
    wb[5].wait_recv()
    wc[6].start()
    wb[6].wait_recv()
    wc[7].start()
    scatter(1)
    input_grad(3)
    gather(0)
    input_grad(5)
    gather(1)
    input_grad(6)
    exchange(0)
    input_grad(7)
    ig_out.start()
    exchange(1)
    halves(0).wait_recv()
    u_out[0].start()
    halves(1).wait_recv()
    u_out[1].start()

    c_send.wait_send()
    for i in range(32):
        x_send(i).wait_send()

    def drain(m, carry):
        z_copy(0, m).wait_send()
        z_copy(1, m).wait_send()
        return carry

    lax.fori_loop(0, 14, drain, 0)
    for copy in wa + wb + wc:
        copy.wait_send()
    for q in range(ROUNDS):
        pair_copy(q).wait_send()
        halves(q).wait_send()
        for k in range(1, 8):
            pieces(q, k).wait_send()
            shares(q, k).wait_send()
        u_out[q].wait()
    nm_out.wait()
    ig_out.wait()


def local(activations, cotangent, key_weight, momentum, selection):
    table = cosine_tile()
    fwd, inv = split_np(np.ascontiguousarray(table.T)), split_np(table)
    hbm, vmem = pl.BlockSpec(memory_space=pl.ANY), pl.BlockSpec(memory_space=pltpu.VMEM)
    dma = pltpu.SemaphoreType.DMA
    return pl.pallas_call(
        kernel,
        out_shape=(
            jax.ShapeDtypeStruct((TOK, D), bf16),
            jax.ShapeDtypeStruct((1, KW, KW), f32),
            jax.ShapeDtypeStruct((KW, KW), f32),
        ),
        in_specs=[hbm] * 5 + [vmem] * 2,
        out_specs=(hbm, hbm, hbm),
        scratch_shapes=[
            pltpu.VMEM((32, 2 * TOK, SUB), bf16),
            pltpu.VMEM((2 * TOK, KW), bf16),
            pltpu.VMEM((2, 14, SUB, KW), bf16),
            pltpu.VMEM((2, 14, SUB, KW), bf16),
            pltpu.VMEM((2, 8, 8, 64, KW), bf16),
            pltpu.VMEM((TOK, D), bf16),
            pltpu.VMEM((KW, KW), f32),
            pltpu.VMEM((KW, KW // 2), jnp.int32),
            pltpu.VMEM((KW, KW), f32),
            pltpu.VMEM((KW, KW), bf16),
            pltpu.VMEM((KW, KW), f32),
            pltpu.VMEM((KW, KW), f32),
            pltpu.VMEM((ROUNDS, RROWS, TILE), bf16),
            pltpu.VMEM((ROUNDS, 8, PIECE, TILE), bf16),
            pltpu.VMEM((ROUNDS, 8, PIECE, TILE), bf16),
            dma((33,)), dma((33,)), dma((32,)),
            dma((2, 14)), dma((2, 14)),
            dma((7,)), dma((7,)), dma((7,)), dma((7,)), dma((8,)), dma((8,)),
            dma((ROUNDS,)), dma((ROUNDS,)),
            dma((ROUNDS, 7)), dma((ROUNDS, 7)), dma((ROUNDS, 7)), dma((ROUNDS, 7)),
            dma((ROUNDS,)), dma((ROUNDS,)),
            dma((4,)), dma((ROUNDS + 2,)),
        ],
        compiler_params=pltpu.CompilerParams(
            collective_id=0, has_side_effects=True, vmem_limit_bytes=48 << 20
        ),
        name="demo_step",
    )(activations, cotangent, key_weight, momentum, selection, jnp.asarray(fwd), jnp.asarray(inv))


def solution(mesh):
    in_specs = (
        P(("rep", "fsdp"), None),
        P(("rep", "fsdp"), None),
        P("fsdp", None),
        P("rep", "fsdp", None),
        P("rep", "fsdp", None),
    )
    out_specs = (P(("rep", "fsdp"), None), P("rep", "fsdp", None), P("fsdp", None))
    return jax.shard_map(local, mesh=mesh, in_specs=in_specs, out_specs=out_specs, check_vma=False)
```

```python
import functools

import jax
import jax.numpy as jnp
import numpy as np
from jax import lax
from jax.experimental import pallas as pl
from jax.experimental.pallas import tpu as pltpu
from jax.sharding import PartitionSpec as P

BLOCK = 64
KEEP = 32
DECAY = 0.9
MESH = pl.DeviceIdType.MESH
TOK = 256
D = 8192
KW = 512
SUB = 128
TILE = 256
ROUNDS = 4
RROWS = KW // ROUNDS
PIECE = RROWS // 8
VMEM_LIMIT = 44 << 20
FLUSH_LIMIT = 1 << 20
f32, bf16 = jnp.float32, jnp.bfloat16


def cosine_tile(flip):
    row = lax.broadcasted_iota(jnp.int32, (TILE, TILE), 1 if flip else 0)
    col = lax.broadcasted_iota(jnp.int32, (TILE, TILE), 0 if flip else 1)
    freq, where_at = row % BLOCK, col % BLOCK
    angle = ((2 * where_at + 1) * freq) % (4 * BLOCK)
    base = (2.0 / BLOCK) ** 0.5 * jnp.cos(angle.astype(f32) * (np.pi / (2 * BLOCK)))
    base = jnp.where(freq == 0, base * 0.5**0.5, base)
    return jnp.where(row // BLOCK == col // BLOCK, base, 0.0)


def split(a):
    hi = a.astype(bf16)
    return hi, (a - hi.astype(f32)).astype(bf16)


def dot(a, b):
    return jnp.dot(a, b, preferred_element_type=f32)


def transform(a, table):
    hi, lo = split(a)
    t_hi, t_lo = table[0], table[1]
    parts = []
    for j in range(a.shape[1] // TILE):
        cols = slice(j * TILE, (j + 1) * TILE)
        parts.append(dot(hi[:, cols], t_hi) + (dot(lo[:, cols], t_hi) + dot(hi[:, cols], t_lo)))
    return parts[0] if len(parts) == 1 else jnp.concatenate(parts, axis=1)


def message(i):
    if i < 4:
        return 4, i // 2 + 2 * (i % 2)
    if i < 20:
        sign, stage, slot = 1 - 2 * (i % 2), (i - 4) // 8, ((i - 4) % 8) // 2
        if stage == 0 and sign > 0:
            slot = (slot + 2) % 4
        return sign * (3 - stage), slot
    return [(1, 0), (-1, 0), (1, 1), (-1, 1), (0, 0), (1, 2), (-1, 2), (0, 1), (1, 3), (-1, 3), (0, 2), (0, 3)][i - 20]


OWN = [next(i for i in range(32) if message(i) == (0, b)) for b in range(4)]
SUMS = [
    (0, None, None), (2, None, None), (4, None, None), (6, None, None), (8, 0, 0), (10, 1, 1), (12, 4, 2),
    (14, 5, 3), (16, 2, 4), (18, 3, 5), (20, 6, 6), (22, 7, 7), (25, 8, 8), (28, 9, 9),
]


def kernel(
    x_ref, c_ref, w_ref, m_ref, s_ref,
    ig_ref, nm_ref, u_ref,
    xb, cb, zs, zr, wg, mv, sv, mk, out, cx, pr, rb, sb, fwd_ref, inv_ref,
    x_ss, x_rs, x_ls, z_ss, z_rs, wa_ss, wa_rs, wb_ss, wb_rs, wd_ss, wd_rs, wc_ss, wc_rs,
    p_ss, p_rs, g_ss, g_rs, h_ss, h_rs, q_ss, q_rs, l_s,
):
    r, f = lax.axis_index("rep"), lax.axis_index("fsdp")
    xh, y, c, xl, z = r // 8, (r // 2) % 4, r % 2, f // 8, f % 8
    chip = xh * 4 + y
    piece = y * 2 + c

    def dev(xh=xh, y=y, c=c, xl=xl, z=z):
        return (xh * 8 + (y % 4) * 2 + c, xl * 8 + z % 8)

    x_mate = dev(xl=1 - xl)
    x_other = dev(xh=1 - xh, xl=1 - xl)
    core_mate = dev(c=1 - c)
    z_to = (dev(z=z + 1), dev(z=z + 7))
    chips = [dev(xh=(xh + k // 4) % 2, y=y + k % 4) for k in range(8)]
    peers = [x_mate, x_other, core_mate, *z_to] + chips[1:]

    def send(src, dst, ss, rs, to):
        return pltpu.make_async_remote_copy(
            src_ref=src, dst_ref=dst, send_sem=ss, recv_sem=rs, device_id=to, device_id_type=MESH
        )

    barrier = pltpu.get_barrier_semaphore()
    for peer in peers:
        pl.semaphore_signal(barrier, inc=1, device_id=peer, device_id_type=MESH)
    pl.semaphore_wait(barrier, len(peers))

    c_send = send(c_ref, cb.at[pl.ds(TOK, TOK)], x_ss.at[32], x_rs.at[32], x_mate)
    c_send.start()

    def column(half, i):
        away, sub = message(i)
        return pl.multiple_of(half * (D // 2) + ((z + away + 8) % 8) * KW + sub * SUB, SUB)

    def x_send(i):
        return send(
            x_ref.at[:, pl.ds(column(1 - xl, i), SUB)], xb.at[i, pl.ds(TOK, TOK)], x_ss.at[i], x_rs.at[i], x_mate
        )

    def x_load(i):
        return pltpu.make_async_copy(
            x_ref.at[:, pl.ds(column(xl, i), SUB)], xb.at[i, pl.ds(0, TOK)], x_ls.at[i]
        )

    w_src = w_ref.at[pl.ds(pl.multiple_of(piece * 64, 64), 64)]
    w_own = pltpu.make_async_copy(w_src, wg.at[xl, z, piece], l_s.at[0])
    c_own = pltpu.make_async_copy(c_ref, cb.at[pl.ds(0, TOK)], l_s.at[1])
    s_own = pltpu.make_async_copy(s_ref.at[0], sv, l_s.at[2])
    m_own = pltpu.make_async_copy(m_ref.at[0], mv, l_s.at[3])

    def ring(way, s):
        slot = wg.at[xl, (z + (8 - s if way == 0 else s)) % 8, piece]
        src = w_src if s == 0 else slot
        return send(src, slot, wa_ss.at[way, s], wa_rs.at[way, s], z_to[way])

    in_plane = (dev(y=y + 1), dev(y=y + 3), x_other)

    def plane(k, n):
        slot = wg.at[xl, (z + 8 - n) % 8, piece]
        return send(w_src if n == 0 else slot, slot, wb_ss.at[k, n], wb_rs.at[k, n], in_plane[k])

    def pass_on(way, s):
        ring(way, s).wait_recv()
        if s < (3 if way == 0 else 2):
            ring(way, s + 1).start()
        for k in range(3):
            plane(k, s + 1 if way == 0 else 7 - s).start()

    for i in range(2):
        x_send(i).start()
    ring(0, 0).start()
    ring(1, 0).start()
    for k in range(3):
        plane(k, 0).start()
    for i in range(2, 32):
        x_send(i).start()
    s_own.start()
    w_own.start()
    c_own.start()
    for i in range(32):
        x_load(i).start()
    m_own.start()
    pass_on(0, 0)
    pass_on(1, 0)

    s_own.wait()
    sel_row = lax.broadcasted_iota(jnp.int32, (KW // 2, KW), 0) // KEEP
    sel_col = lax.broadcasted_iota(jnp.int32, (KW // 2, KW), 1)
    spread = [
        jnp.where((sel_row == sel_col // BLOCK) & ((sel_col % BLOCK) // 16 == g), 1.0, 0.0).astype(bf16)
        for g in range(4)
    ]
    bit = lax.broadcasted_iota(jnp.int32, (SUB, KW), 1) % 16

    def mask_rows(b, carry):
        rows = pl.ds(pl.multiple_of(b * SUB, SUB), SUB)
        sel = sv[rows, :]
        power = jnp.left_shift(1, sel % 16).astype(f32)
        total = jnp.zeros((SUB, KW), f32)
        for g in range(4):
            total += dot(jnp.where(sel // 16 == g, power, 0.0).astype(bf16), spread[g])
        mk[rows, :] = (jnp.right_shift(total.astype(jnp.int32), bit) % 2).astype(f32)
        return carry

    lax.fori_loop(0, KW // SUB, mask_rows, 0)
    pass_on(0, 1)
    pass_on(1, 1)
    fwd_ref[0], fwd_ref[1] = split(cosine_tile(True))
    inv_ref[0], inv_ref[1] = split(cosine_tile(False))
    w_own.wait()
    c_own.wait()
    m_own.wait()

    def product(i):
        pltpu.make_async_copy(x_ref.at[:, pl.ds(0, SUB)], xb.at[i, pl.ds(0, TOK)], x_ls.at[i]).wait()
        send(xb.at[i, pl.ds(0, TOK)], xb.at[i, pl.ds(TOK, TOK)], x_ss.at[i], x_rs.at[i], x_mate).wait_recv()
        return lax.dot_general(xb[i], cb[...], (((0,), (0,)), ((), ())), preferred_element_type=f32)

    def z_copy(way, m):
        return send(zs.at[way, m], zr.at[way, m], z_ss.at[way, m], z_rs.at[way, m], z_to[way])

    def step(way, m, i, before):
        total = product(i)
        if before is not None:
            z_copy(way, before).wait_recv()
            total += zr[way, before].astype(f32)
        zs[way, m] = total.astype(bf16)
        z_copy(way, m).start()

    def steps(m):
        first, *before = SUMS[m]
        for way in range(2):
            step(way, m, first + way, before[way])

    def group(x_side, y_side, core):
        return wg.at[x_side, :, (y_side % 4) * 2 + core]

    def later(n, at, to):
        return send(at, at, wd_ss.at[n], wd_rs.at[n], to)

    def half_group(x_side, y_side, h):
        return wg.at[x_side, pl.ds(4 * h, 4), (y_side % 4) * 2 + c]

    wd = [
        later(0, group(xl, y, c), dev(y=y + 2)),
        later(1, group(1 - xl, y, c), dev(y=y + 3)),
        later(2, half_group(xl, y + 3, 0), x_other),
        later(3, half_group(xl, y + 3, 1), x_other),
        later(4, half_group(1 - xl, y + 3, 0), dev(y=y + 1)),
        later(5, half_group(1 - xl, y + 3, 1), dev(y=y + 1)),
    ]
    groups = [(xl, y), (xl, y + 3), (xl, y + 1), (1 - xl, y), (xl, y + 2), (1 - xl, y + 3), (1 - xl, y + 1), (1 - xl, y + 2)]
    wc = [
        send(group(*g, c), group(*g, c), wc_ss.at[k], wc_rs.at[k], core_mate) for k, g in enumerate(groups)
    ]

    def input_grad(k):
        half, place = groups[k]
        place = place % 4
        wc[k].wait_recv()

        def body(zz, carry):
            rows = wg[half, zz, pl.ds(place * 2, 2)].reshape(SUB, KW)
            col = pl.multiple_of(half * (D // 2) + zz * KW + place * SUB, SUB)
            ig_ref[:, pl.ds(col, SUB)] = lax.dot_general(
                cb[0:TOK], rows, (((1,), (1,)), ((), ())), preferred_element_type=f32
            ).astype(bf16)
            return carry

        lax.fori_loop(0, 8, body, 0)

    mine = pl.ds(pl.multiple_of(c * TILE, TILE), TILE)
    theirs = pl.ds(pl.multiple_of((1 - c) * TILE, TILE), TILE)
    span = [pl.ds(q * RROWS, RROWS) for q in range(ROUNDS)]
    own_piece = [pl.ds(pl.multiple_of(q * RROWS + chip * PIECE, PIECE), PIECE) for q in range(ROUNDS)]

    def pair(q):
        return send(out.at[span[q], theirs], cx.at[q], p_ss.at[q], p_rs.at[q], core_mate)

    def pieces(q, k):
        to = ((xh + k // 4) % 2) * 4 + (y + k) % 4
        return send(pr.at[q, to], rb.at[q, chip], g_ss.at[q, k - 1], g_rs.at[q, k - 1], chips[k])

    def shares(q, k):
        at = sb.at[own_piece[q], mine]
        return send(at, at, h_ss.at[q, k - 1], h_rs.at[q, k - 1], chips[k])

    def halves(q):
        at = sb.at[span[q], mine]
        return send(at, at, q_ss.at[q], q_rs.at[q], core_mate)

    def finish(b):
        rows = pl.ds(b * SUB, SUB)
        total = product(OWN[b]) + DECAY * mv[rows, :]
        z_copy(0, 10 + b).wait_recv()
        z_copy(1, 10 + b).wait_recv()
        total += zr[0, 10 + b].astype(f32) + zr[1, 10 + b].astype(f32)
        retained = mk[rows, :] * transform(total, fwd_ref)
        out[rows, :] = retained.astype(bf16)
        pair(b).start()
        nm_ref[rows, :] = total
        mk[rows, :] = retained

    def renew(b):
        rows = pl.ds(b * SUB, SUB)
        nm_ref[rows, :] -= transform(mk[rows, :], inv_ref)

    def scatter(q):
        pair(q).wait_recv()
        both = out[span[q], mine].astype(f32) + cx[q].astype(f32)
        pr[q] = both.astype(bf16).reshape(8, PIECE, TILE)
        for k in range(1, 8):
            pieces(q, k).start()

    def gather(q):
        rb[q, chip] = pr[q, chip]
        for k in range(1, 8):
            pieces(q, k).wait_recv()
        sb[own_piece[q], mine] = jnp.sum(rb[q].astype(f32), axis=0).astype(bf16)
        for k in range(1, 8):
            shares(q, k).start()

    def exchange(q):
        for k in range(1, 8):
            shares(q, k).wait_recv()
        halves(q).start()

    def result(q):
        halves(q).wait_recv()
        both = sb[span[q], :]
        for j in range(KW // TILE):
            cols = slice(j * TILE, (j + 1) * TILE)
            u_ref[span[q], cols] = (dot(both[:, cols], inv_ref[0]) + dot(both[:, cols], inv_ref[1])) * (1.0 / 16.0)

    c_send.wait_recv()
    steps(0)
    pass_on(0, 2)
    pass_on(1, 2)
    steps(1)
    steps(2)
    pass_on(0, 3)
    wd[0].start()
    wc[0].start()
    steps(3)
    input_grad(0)
    steps(4)
    for k in range(3):
        for n in range(8):
            plane(k, n).wait_recv()
    for k in (2, 3, 1):
        wd[k].start()
    for k in (3, 1, 2):
        wc[k].start()
    steps(5)
    input_grad(3)
    steps(6)
    input_grad(1)
    steps(7)
    wd[2].wait_recv()
    wd[4].start()
    steps(8)
    input_grad(2)
    steps(9)
    wd[3].wait_recv()
    wd[5].start()
    wc[5].start()
    wd[0].wait_recv()
    wc[4].start()
    steps(10)
    input_grad(5)
    steps(11)
    input_grad(4)
    finish(0)
    steps(12)
    wd[1].wait_recv()
    wc[6].start()
    finish(1)
    steps(13)
    finish(2)
    scatter(0)
    scatter(1)
    finish(3)
    scatter(2)
    wd[4].wait_recv()
    wd[5].wait_recv()
    wc[7].start()
    scatter(3)
    gather(0)
    gather(1)
    input_grad(6)
    gather(2)
    gather(3)
    renew(0)
    renew(1)
    exchange(0)
    exchange(1)
    input_grad(7)
    exchange(2)
    renew(2)
    renew(3)
    exchange(3)
    for q in range(ROUNDS):
        result(q)

    c_send.wait_send()
    for i in range(32):
        x_send(i).wait_send()

    def drain(m, carry):
        z_copy(0, m).wait_send()
        z_copy(1, m).wait_send()
        return carry

    lax.fori_loop(0, 14, drain, 0)
    for s in range(4):
        ring(0, s).wait_send()
    for s in range(3):
        ring(1, s).wait_send()
    for k in range(3):
        for n in range(8):
            plane(k, n).wait_send()
    for copy in wd + wc:
        copy.wait_send()
    for q in range(ROUNDS):
        pair(q).wait_send()
        halves(q).wait_send()
        for k in range(1, 8):
            pieces(q, k).wait_send()
            shares(q, k).wait_send()


def flush(ig_ref, nm_ref, u_ref, ig_out, nm_out, u_out, sems):
    copies = [
        pltpu.make_async_copy(ig_ref.at[pl.ds(k * 64, 64)], ig_out.at[pl.ds(k * 64, 64)], sems.at[k]) for k in range(4)
    ]
    copies += [pltpu.make_async_copy(nm_ref, nm_out.at[0], sems.at[4]), pltpu.make_async_copy(u_ref, u_out, sems.at[5])]
    for copy in copies:
        copy.start()
    for copy in copies:
        copy.wait()


def local(activations, cotangent, key_weight, momentum, selection):
    hbm, vmem = pl.BlockSpec(memory_space=pltpu.HBM), pl.BlockSpec(memory_space=pltpu.VMEM)
    dma = pltpu.SemaphoreType.DMA
    outs = pl.pallas_call(
        kernel,
        out_shape=(
            jax.ShapeDtypeStruct((TOK, D), bf16),
            jax.ShapeDtypeStruct((KW, KW), f32),
            jax.ShapeDtypeStruct((KW, KW), f32),
        ),
        in_specs=[hbm] * 5,
        out_specs=(vmem, vmem, vmem),
        scratch_shapes=[
            pltpu.VMEM((32, 2 * TOK, SUB), bf16),
            pltpu.VMEM((2 * TOK, KW), bf16),
            pltpu.VMEM((2, 14, SUB, KW), bf16),
            pltpu.VMEM((2, 14, SUB, KW), bf16),
            pltpu.VMEM((2, 8, 8, 64, KW), bf16),
            pltpu.VMEM((KW, KW), f32),
            pltpu.VMEM((KW, KW // 2), jnp.int32),
            pltpu.VMEM((KW, KW), f32),
            pltpu.VMEM((KW, KW), bf16),
            pltpu.VMEM((ROUNDS, RROWS, TILE), bf16),
            pltpu.VMEM((ROUNDS, 8, PIECE, TILE), bf16),
            pltpu.VMEM((ROUNDS, 8, PIECE, TILE), bf16),
            pltpu.VMEM((KW, KW), bf16),
            pltpu.VMEM((2, TILE, TILE), bf16),
            pltpu.VMEM((2, TILE, TILE), bf16),
            dma((33,)), dma((33,)), dma((32,)),
            dma((2, 14)), dma((2, 14)),
            dma((2, 4)), dma((2, 4)), dma((3, 8)), dma((3, 8)), dma((6,)), dma((6,)), dma((8,)), dma((8,)),
            dma((ROUNDS,)), dma((ROUNDS,)),
            dma((ROUNDS, 7)), dma((ROUNDS, 7)), dma((ROUNDS, 7)), dma((ROUNDS, 7)),
            dma((ROUNDS,)), dma((ROUNDS,)), dma((4,)),
        ],
        compiler_params=pltpu.CompilerParams(
            collective_id=0, has_side_effects=True, vmem_limit_bytes=VMEM_LIMIT
        ),
        name="demo_step",
    )(*(pltpu.with_memory_space_constraint(a, pltpu.HBM) for a in (activations, cotangent, key_weight, momentum, selection)))
    return pl.pallas_call(
        flush,
        out_shape=(
            jax.ShapeDtypeStruct((TOK, D), bf16),
            jax.ShapeDtypeStruct((1, KW, KW), f32),
            jax.ShapeDtypeStruct((KW, KW), f32),
        ),
        in_specs=[vmem] * 3,
        out_specs=(hbm, hbm, hbm),
        scratch_shapes=[dma((6,))],
        compiler_params=pltpu.CompilerParams(vmem_limit_bytes=FLUSH_LIMIT),
        name="flush",
    )(*outs)


def solution(mesh):
    in_specs = (
        P(("rep", "fsdp"), None),
        P(("rep", "fsdp"), None),
        P("fsdp", None),
        P("rep", "fsdp", None),
        P("rep", "fsdp", None),
    )
    out_specs = (P(("rep", "fsdp"), None), P("rep", "fsdp", None), P("fsdp", None))
    return jax.shard_map(local, mesh=mesh, in_specs=in_specs, out_specs=out_specs, check_vma=False)
```

```python
import functools

import jax
import jax.numpy as jnp
import numpy as np
from jax import lax
from jax.experimental import pallas as pl
from jax.experimental.pallas import tpu as pltpu
from jax.sharding import PartitionSpec as P

BLOCK = 64
KEEP = 32
DECAY = 0.9
MESH = pl.DeviceIdType.MESH
TOK = 256
D = 8192
KW = 512
SUB = 128
TILE = 256
ROUNDS = 4
RROWS = KW // ROUNDS
PIECE = RROWS // 8
VMEM_LIMIT = 44 << 20
FLUSH_LIMIT = 1 << 20
f32, bf16 = jnp.float32, jnp.bfloat16


def cosine_tile(flip):
    row = lax.broadcasted_iota(jnp.int32, (TILE, TILE), 1 if flip else 0)
    col = lax.broadcasted_iota(jnp.int32, (TILE, TILE), 0 if flip else 1)
    freq, where_at = row % BLOCK, col % BLOCK
    angle = ((2 * where_at + 1) * freq) % (4 * BLOCK)
    base = (2.0 / BLOCK) ** 0.5 * jnp.cos(angle.astype(f32) * (np.pi / (2 * BLOCK)))
    base = jnp.where(freq == 0, base * 0.5**0.5, base)
    return jnp.where(row // BLOCK == col // BLOCK, base, 0.0)


def split(a):
    hi = a.astype(bf16)
    return hi, (a - hi.astype(f32)).astype(bf16)


def dot(a, b):
    return jnp.dot(a, b, preferred_element_type=f32)


def transform(a, table):
    hi, lo = split(a)
    t_hi, t_lo = table[0], table[1]
    parts = []
    for j in range(a.shape[1] // TILE):
        cols = slice(j * TILE, (j + 1) * TILE)
        parts.append(dot(hi[:, cols], t_hi) + (dot(lo[:, cols], t_hi) + dot(hi[:, cols], t_lo)))
    return parts[0] if len(parts) == 1 else jnp.concatenate(parts, axis=1)


def message(i):
    if i < 4:
        return 4, i // 2 + 2 * (i % 2)
    if i < 20:
        sign, stage, slot = 1 - 2 * (i % 2), (i - 4) // 8, ((i - 4) % 8) // 2
        if stage == 0 and sign > 0:
            slot = (slot + 2) % 4
        return sign * (3 - stage), slot
    return [(1, 0), (-1, 0), (1, 1), (-1, 1), (1, 2), (-1, 2), (1, 3), (-1, 3), (0, 0), (0, 1), (0, 2), (0, 3)][i - 20]


OWN = [next(i for i in range(32) if message(i) == (0, b)) for b in range(4)]
SUMS = [
    (0, None, None), (2, None, None), (4, None, None), (6, None, None), (8, 0, 0), (10, 1, 1), (12, 4, 2),
    (14, 5, 3), (16, 2, 4), (18, 3, 5), (20, 6, 6), (22, 7, 7), (24, 8, 8), (26, 9, 9),
]


def kernel(
    x_ref, c_ref, w_ref, m_ref, s_ref,
    ig_ref, nm_ref, u_ref,
    xb, cb, zs, zr, wg, mv, sv, mk, out, cx, pr, rb, sb, fwd_ref, inv_ref,
    x_ss, x_rs, x_ls, z_ss, z_rs, wa_ss, wa_rs, wb_ss, wb_rs, wd_ss, wd_rs, wc_ss, wc_rs,
    p_ss, p_rs, g_ss, g_rs, h_ss, h_rs, q_ss, q_rs, l_s,
):
    r, f = lax.axis_index("rep"), lax.axis_index("fsdp")
    xh, y, c, xl, z = r // 8, (r // 2) % 4, r % 2, f // 8, f % 8
    chip = xh * 4 + y
    piece = y * 2 + c

    def dev(xh=xh, y=y, c=c, xl=xl, z=z):
        return (xh * 8 + (y % 4) * 2 + c, xl * 8 + z % 8)

    x_mate = dev(xl=1 - xl)
    x_other = dev(xh=1 - xh, xl=1 - xl)
    core_mate = dev(c=1 - c)
    z_to = (dev(z=z + 1), dev(z=z + 7))
    chips = [dev(xh=(xh + k // 4) % 2, y=y + k % 4) for k in range(8)]
    peers = [x_mate, x_other, core_mate, *z_to] + chips[1:]

    def send(src, dst, ss, rs, to):
        return pltpu.make_async_remote_copy(
            src_ref=src, dst_ref=dst, send_sem=ss, recv_sem=rs, device_id=to, device_id_type=MESH
        )

    barrier = pltpu.get_barrier_semaphore()
    for peer in peers:
        pl.semaphore_signal(barrier, inc=1, device_id=peer, device_id_type=MESH)
    pl.semaphore_wait(barrier, len(peers))

    c_send = send(c_ref, cb.at[pl.ds(TOK, TOK)], x_ss.at[32], x_rs.at[32], x_mate)
    c_send.start()

    def column(half, i):
        away, sub = message(i)
        return pl.multiple_of(half * (D // 2) + ((z + away + 8) % 8) * KW + sub * SUB, SUB)

    def x_send(i):
        return send(
            x_ref.at[:, pl.ds(column(1 - xl, i), SUB)], xb.at[i, pl.ds(TOK, TOK)], x_ss.at[i], x_rs.at[i], x_mate
        )

    def x_load(i):
        return pltpu.make_async_copy(
            x_ref.at[:, pl.ds(column(xl, i), SUB)], xb.at[i, pl.ds(0, TOK)], x_ls.at[i]
        )

    w_src = w_ref.at[pl.ds(pl.multiple_of(piece * 64, 64), 64)]
    w_own = pltpu.make_async_copy(w_src, wg.at[xl, z, piece], l_s.at[0])
    c_own = pltpu.make_async_copy(c_ref, cb.at[pl.ds(0, TOK)], l_s.at[1])
    s_own = pltpu.make_async_copy(s_ref.at[0], sv, l_s.at[2])
    m_own = pltpu.make_async_copy(m_ref.at[0], mv, l_s.at[3])

    def ring(way, s):
        slot = wg.at[xl, (z + (8 - s if way == 0 else s)) % 8, piece]
        src = w_src if s == 0 else slot
        return send(src, slot, wa_ss.at[way, s], wa_rs.at[way, s], z_to[way])

    in_plane = (dev(y=y + 1), dev(y=y + 3), x_other)

    def plane(k, n):
        slot = wg.at[xl, (z + 8 - n) % 8, piece]
        return send(w_src if n == 0 else slot, slot, wb_ss.at[k, n], wb_rs.at[k, n], in_plane[k])

    def pass_on(way, s):
        ring(way, s).wait_recv()
        if s < (3 if way == 0 else 2):
            ring(way, s + 1).start()
        for k in range(3):
            plane(k, s + 1 if way == 0 else 7 - s).start()

    for i in range(2):
        x_send(i).start()
    ring(0, 0).start()
    ring(1, 0).start()
    for k in range(3):
        plane(k, 0).start()
    for i in range(2, 32):
        x_send(i).start()
    s_own.start()
    w_own.start()
    c_own.start()
    for i in range(32):
        x_load(i).start()
    m_own.start()
    pass_on(0, 0)
    pass_on(1, 0)

    s_own.wait()
    sel_row = lax.broadcasted_iota(jnp.int32, (KW // 2, KW), 0) // KEEP
    sel_col = lax.broadcasted_iota(jnp.int32, (KW // 2, KW), 1)
    spread = [
        jnp.where((sel_row == sel_col // BLOCK) & ((sel_col % BLOCK) // 16 == g), 1.0, 0.0).astype(bf16)
        for g in range(4)
    ]
    bit = lax.broadcasted_iota(jnp.int32, (SUB, KW), 1) % 16

    def mask_rows(b, carry):
        rows = pl.ds(pl.multiple_of(b * SUB, SUB), SUB)
        sel = sv[rows, :]
        power = jnp.left_shift(1, sel % 16).astype(f32)
        total = jnp.zeros((SUB, KW), f32)
        for g in range(4):
            total += dot(jnp.where(sel // 16 == g, power, 0.0).astype(bf16), spread[g])
        mk[rows, :] = (jnp.right_shift(total.astype(jnp.int32), bit) % 2).astype(f32)
        return carry

    lax.fori_loop(0, KW // SUB, mask_rows, 0)
    pass_on(0, 1)
    pass_on(1, 1)
    fwd_ref[0], fwd_ref[1] = split(cosine_tile(True))
    inv_ref[0], inv_ref[1] = split(cosine_tile(False))
    w_own.wait()
    c_own.wait()
    m_own.wait()

    def product(i):
        pltpu.make_async_copy(x_ref.at[:, pl.ds(0, SUB)], xb.at[i, pl.ds(0, TOK)], x_ls.at[i]).wait()
        send(xb.at[i, pl.ds(0, TOK)], xb.at[i, pl.ds(TOK, TOK)], x_ss.at[i], x_rs.at[i], x_mate).wait_recv()
        return lax.dot_general(xb[i], cb[...], (((0,), (0,)), ((), ())), preferred_element_type=f32)

    def z_copy(way, m):
        return send(zs.at[way, m], zr.at[way, m], z_ss.at[way, m], z_rs.at[way, m], z_to[way])

    def step(way, m, i, before):
        total = product(i)
        if before is not None:
            z_copy(way, before).wait_recv()
            total += zr[way, before].astype(f32)
        zs[way, m] = total.astype(bf16)
        z_copy(way, m).start()

    def steps(m):
        first, *before = SUMS[m]
        for way in range(2):
            step(way, m, first + way, before[way])

    def group(x_side, y_side, core):
        return wg.at[x_side, :, (y_side % 4) * 2 + core]

    def later(n, at, to):
        return send(at, at, wd_ss.at[n], wd_rs.at[n], to)

    def half_group(x_side, y_side, h):
        return wg.at[x_side, pl.ds(4 * h, 4), (y_side % 4) * 2 + c]

    wd = [
        later(0, group(xl, y, c), dev(y=y + 2)),
        later(1, group(1 - xl, y, c), dev(y=y + 3)),
        later(2, half_group(xl, y + 3, 0), x_other),
        later(3, half_group(xl, y + 3, 1), x_other),
        later(4, half_group(1 - xl, y + 3, 0), dev(y=y + 1)),
        later(5, half_group(1 - xl, y + 3, 1), dev(y=y + 1)),
    ]
    groups = [(xl, y), (xl, y + 3), (xl, y + 1), (1 - xl, y), (xl, y + 2), (1 - xl, y + 3), (1 - xl, y + 1), (1 - xl, y + 2)]
    wc = [
        send(group(*g, c), group(*g, c), wc_ss.at[k], wc_rs.at[k], core_mate) for k, g in enumerate(groups)
    ]

    def input_grad(k):
        half, place = groups[k]
        place = place % 4
        wc[k].wait_recv()

        for first in range(0, 8, 4):
            rows = wg[half, pl.ds(first, 4), pl.ds(place * 2, 2)].reshape(4 * SUB, KW)
            grads = lax.dot_general(
                cb[0:TOK], rows, (((1,), (1,)), ((), ())), preferred_element_type=f32
            ).astype(bf16)
            for n in range(4):
                col = pl.multiple_of(half * (D // 2) + (first + n) * KW + place * SUB, SUB)
                ig_ref[:, pl.ds(col, SUB)] = grads[:, n * SUB : (n + 1) * SUB]

    mine = pl.ds(pl.multiple_of(c * TILE, TILE), TILE)
    theirs = pl.ds(pl.multiple_of((1 - c) * TILE, TILE), TILE)
    span = [pl.ds(q * RROWS, RROWS) for q in range(ROUNDS)]
    own_piece = [pl.ds(pl.multiple_of(q * RROWS + chip * PIECE, PIECE), PIECE) for q in range(ROUNDS)]

    def pair(q):
        return send(out.at[span[q], theirs], cx.at[q], p_ss.at[q], p_rs.at[q], core_mate)

    def pieces(q, k):
        to = ((xh + k // 4) % 2) * 4 + (y + k) % 4
        return send(pr.at[q, to], rb.at[q, chip], g_ss.at[q, k - 1], g_rs.at[q, k - 1], chips[k])

    def shares(q, k):
        at = sb.at[own_piece[q], mine]
        return send(at, at, h_ss.at[q, k - 1], h_rs.at[q, k - 1], chips[k])

    def halves(q):
        at = sb.at[span[q], mine]
        return send(at, at, q_ss.at[q], q_rs.at[q], core_mate)

    def finish(b):
        rows = pl.ds(b * SUB, SUB)
        total = product(OWN[b]) + DECAY * mv[rows, :]
        z_copy(0, 10 + b).wait_recv()
        z_copy(1, 10 + b).wait_recv()
        total += zr[0, 10 + b].astype(f32) + zr[1, 10 + b].astype(f32)
        retained = mk[rows, :] * transform(total, fwd_ref)
        out[rows, :] = retained.astype(bf16)
        pair(b).start()
        nm_ref[rows, :] = total
        mk[rows, :] = retained

    def renew(b):
        rows = pl.ds(b * SUB, SUB)
        nm_ref[rows, :] -= transform(mk[rows, :], inv_ref)

    def scatter(q):
        pair(q).wait_recv()
        both = out[span[q], mine].astype(f32) + cx[q].astype(f32)
        pr[q] = both.astype(bf16).reshape(8, PIECE, TILE)
        for k in range(1, 8):
            pieces(q, k).start()

    def gather(q):
        rb[q, chip] = pr[q, chip]
        for k in range(1, 8):
            pieces(q, k).wait_recv()
        sb[own_piece[q], mine] = jnp.sum(rb[q].astype(f32), axis=0).astype(bf16)
        for k in range(1, 8):
            shares(q, k).start()

    def exchange(q):
        for k in range(1, 8):
            shares(q, k).wait_recv()
        halves(q).start()

    def result(q):
        halves(q).wait_recv()
        both = sb[span[q], :]
        for j in range(KW // TILE):
            cols = slice(j * TILE, (j + 1) * TILE)
            u_ref[span[q], cols] = (dot(both[:, cols], inv_ref[0]) + dot(both[:, cols], inv_ref[1])) * (1.0 / 16.0)

    c_send.wait_recv()
    steps(0)
    pass_on(0, 2)
    pass_on(1, 2)
    steps(1)
    steps(2)
    pass_on(0, 3)
    wd[0].start()
    wc[0].start()
    steps(3)
    input_grad(0)
    steps(4)
    for k in range(3):
        for n in range(8):
            plane(k, n).wait_recv()
    for k in (2, 3, 1):
        wd[k].start()
    for k in (3, 1, 2):
        wc[k].start()
    steps(5)
    input_grad(3)
    steps(6)
    input_grad(1)
    steps(7)
    wd[2].wait_recv()
    wd[4].start()
    steps(8)
    input_grad(2)
    steps(9)
    wd[3].wait_recv()
    wd[5].start()
    wc[5].start()
    wd[0].wait_recv()
    wc[4].start()
    steps(10)
    input_grad(5)
    steps(11)
    input_grad(4)
    steps(12)
    steps(13)
    wd[1].wait_recv()
    wc[6].start()
    finish(0)
    finish(1)
    scatter(0)
    finish(2)
    scatter(1)
    finish(3)
    scatter(2)
    wd[4].wait_recv()
    wd[5].wait_recv()
    wc[7].start()
    scatter(3)
    c_send.wait_send()
    for i in range(32):
        x_send(i).wait_send()
    for s in range(4):
        ring(0, s).wait_send()
    for s in range(3):
        ring(1, s).wait_send()
    gather(0)
    gather(1)
    for k in range(3):
        for n in range(8):
            plane(k, n).wait_send()
    input_grad(6)
    gather(2)
    gather(3)
    renew(0)
    renew(1)

    def drain(m, carry):
        z_copy(0, m).wait_send()
        z_copy(1, m).wait_send()
        return carry

    lax.fori_loop(0, 14, drain, 0)
    for copy in wd:
        copy.wait_send()
    exchange(0)
    exchange(1)
    input_grad(7)
    renew(2)
    renew(3)
    for copy in wc:
        copy.wait_send()
    for q in range(ROUNDS):
        pair(q).wait_send()
        for k in range(1, 8):
            pieces(q, k).wait_send()
    exchange(2)
    result(0)
    result(1)
    for q in range(2):
        for k in range(1, 8):
            shares(q, k).wait_send()
    exchange(3)
    result(2)
    for k in range(1, 8):
        shares(2, k).wait_send()
    result(3)
    for k in range(1, 8):
        shares(3, k).wait_send()
    for q in range(ROUNDS):
        halves(q).wait_send()


def flush(ig_ref, nm_ref, u_ref, ig_out, nm_out, u_out, sems):
    copies = [
        pltpu.make_async_copy(ig_ref.at[pl.ds(k * 64, 64)], ig_out.at[pl.ds(k * 64, 64)], sems.at[k]) for k in range(4)
    ]
    copies += [pltpu.make_async_copy(nm_ref, nm_out.at[0], sems.at[4]), pltpu.make_async_copy(u_ref, u_out, sems.at[5])]
    for copy in copies:
        copy.start()
    for copy in copies:
        copy.wait()


def local(activations, cotangent, key_weight, momentum, selection):
    hbm, vmem = pl.BlockSpec(memory_space=pltpu.HBM), pl.BlockSpec(memory_space=pltpu.VMEM)
    dma = pltpu.SemaphoreType.DMA
    outs = pl.pallas_call(
        kernel,
        out_shape=(
            jax.ShapeDtypeStruct((TOK, D), bf16),
            jax.ShapeDtypeStruct((KW, KW), f32),
            jax.ShapeDtypeStruct((KW, KW), f32),
        ),
        in_specs=[hbm] * 5,
        out_specs=(vmem, vmem, vmem),
        scratch_shapes=[
            pltpu.VMEM((32, 2 * TOK, SUB), bf16),
            pltpu.VMEM((2 * TOK, KW), bf16),
            pltpu.VMEM((2, 14, SUB, KW), bf16),
            pltpu.VMEM((2, 14, SUB, KW), bf16),
            pltpu.VMEM((2, 8, 8, 64, KW), bf16),
            pltpu.VMEM((KW, KW), f32),
            pltpu.VMEM((KW, KW // 2), jnp.int32),
            pltpu.VMEM((KW, KW), f32),
            pltpu.VMEM((KW, KW), bf16),
            pltpu.VMEM((ROUNDS, RROWS, TILE), bf16),
            pltpu.VMEM((ROUNDS, 8, PIECE, TILE), bf16),
            pltpu.VMEM((ROUNDS, 8, PIECE, TILE), bf16),
            pltpu.VMEM((KW, KW), bf16),
            pltpu.VMEM((2, TILE, TILE), bf16),
            pltpu.VMEM((2, TILE, TILE), bf16),
            dma((33,)), dma((33,)), dma((32,)),
            dma((2, 14)), dma((2, 14)),
            dma((2, 4)), dma((2, 4)), dma((3, 8)), dma((3, 8)), dma((6,)), dma((6,)), dma((8,)), dma((8,)),
            dma((ROUNDS,)), dma((ROUNDS,)),
            dma((ROUNDS, 7)), dma((ROUNDS, 7)), dma((ROUNDS, 7)), dma((ROUNDS, 7)),
            dma((ROUNDS,)), dma((ROUNDS,)), dma((4,)),
        ],
        compiler_params=pltpu.CompilerParams(
            collective_id=0, has_side_effects=True, vmem_limit_bytes=VMEM_LIMIT
        ),
        name="demo_step",
    )(*(pltpu.with_memory_space_constraint(a, pltpu.HBM) for a in (activations, cotangent, key_weight, momentum, selection)))
    return pl.pallas_call(
        flush,
        out_shape=(
            jax.ShapeDtypeStruct((TOK, D), bf16),
            jax.ShapeDtypeStruct((1, KW, KW), f32),
            jax.ShapeDtypeStruct((KW, KW), f32),
        ),
        in_specs=[vmem] * 3,
        out_specs=(hbm, hbm, hbm),
        scratch_shapes=[dma((6,))],
        compiler_params=pltpu.CompilerParams(vmem_limit_bytes=FLUSH_LIMIT),
        name="flush",
    )(*outs)


def solution(mesh):
    in_specs = (
        P(("rep", "fsdp"), None),
        P(("rep", "fsdp"), None),
        P("fsdp", None),
        P("rep", "fsdp", None),
        P("rep", "fsdp", None),
    )
    out_specs = (P(("rep", "fsdp"), None), P("rep", "fsdp", None), P("fsdp", None))
    return jax.shard_map(local, mesh=mesh, in_specs=in_specs, out_specs=out_specs, check_vma=False)
```

```python
import functools

import jax
import jax.numpy as jnp
import numpy as np
from jax import lax
from jax.experimental import pallas as pl
from jax.experimental.pallas import tpu as pltpu
from jax.sharding import PartitionSpec as P

BLOCK = 64
KEEP = 32
DECAY = 0.9
MESH = pl.DeviceIdType.MESH
TOK = 256
D = 8192
KW = 512
SUB = 128
TILE = 256
ROUNDS = ((0, 2), (2, 1), (3, 1))
N_ROUNDS = len(ROUNDS)
VMEM_LIMIT = 44 << 20
FLUSH_LIMIT = 1 << 20
f32, bf16 = jnp.float32, jnp.bfloat16


def cosine_tile(flip):
    row = lax.broadcasted_iota(jnp.int32, (TILE, TILE), 1 if flip else 0)
    col = lax.broadcasted_iota(jnp.int32, (TILE, TILE), 0 if flip else 1)
    freq, where_at = row % BLOCK, col % BLOCK
    angle = ((2 * where_at + 1) * freq) % (4 * BLOCK)
    base = (2.0 / BLOCK) ** 0.5 * jnp.cos(angle.astype(f32) * (np.pi / (2 * BLOCK)))
    base = jnp.where(freq == 0, base * 0.5**0.5, base)
    return jnp.where(row // BLOCK == col // BLOCK, base, 0.0)


def split(a):
    hi = a.astype(bf16)
    return hi, (a - hi.astype(f32)).astype(bf16)


def dot(a, b):
    return jnp.dot(a, b, preferred_element_type=f32)


def transform(a, table):
    hi, lo = split(a)
    t_hi, t_lo = table[0], table[1]
    parts = []
    for j in range(a.shape[1] // TILE):
        cols = slice(j * TILE, (j + 1) * TILE)
        parts.append(dot(hi[:, cols], t_hi) + (dot(lo[:, cols], t_hi) + dot(hi[:, cols], t_lo)))
    return parts[0] if len(parts) == 1 else jnp.concatenate(parts, axis=1)


def message(i):
    if i < 4:
        return 4, i // 2 + 2 * (i % 2)
    if i < 20:
        sign, stage, slot = 1 - 2 * (i % 2), (i - 4) // 8, ((i - 4) % 8) // 2
        if stage == 0 and sign > 0:
            slot = (slot + 2) % 4
        return sign * (3 - stage), slot
    return [(1, 0), (-1, 0), (1, 1), (-1, 1), (1, 2), (-1, 2), (1, 3), (-1, 3), (0, 0), (0, 1), (0, 2), (0, 3)][i - 20]


FAR = (6, 5, 7, 4, 2, 1, 3)
OWN = [next(i for i in range(32) if message(i) == (0, b)) for b in range(4)]
SUMS = [
    (0, None, None), (2, None, None), (4, None, None), (6, None, None), (8, 0, 0), (10, 1, 1), (12, 4, 2),
    (14, 5, 3), (16, 2, 4), (18, 3, 5), (20, 6, 6), (22, 7, 7), (24, 8, 8), (26, 9, 9),
]


def kernel(
    x_ref, c_ref, w_ref, m_ref, s_ref,
    ig_ref, nm_ref, u_ref,
    xb, cb, zs, zr, wg, mv, sv, mk, out, cx, pr, rb, sb, fwd_ref, inv_ref,
    x_ss, x_rs, x_ls, z_ss, z_rs, wa_ss, wa_rs, wb_ss, wb_rs, wd_ss, wd_rs, wc_ss, wc_rs,
    p_ss, p_rs, g_ss, g_rs, h_ss, h_rs, q_ss, q_rs, l_s,
):
    r, f = lax.axis_index("rep"), lax.axis_index("fsdp")
    xh, y, c, xl, z = r // 8, (r // 2) % 4, r % 2, f // 8, f % 8
    chip = xh * 4 + y
    piece = y * 2 + c

    def dev(xh=xh, y=y, c=c, xl=xl, z=z):
        return (xh * 8 + (y % 4) * 2 + c, xl * 8 + z % 8)

    x_mate = dev(xl=1 - xl)
    x_other = dev(xh=1 - xh, xl=1 - xl)
    core_mate = dev(c=1 - c)
    z_to = (dev(z=z + 1), dev(z=z + 7))
    chips = [dev(xh=(xh + k // 4) % 2, y=y + k % 4) for k in range(8)]
    peers = [x_mate, x_other, core_mate, *z_to] + chips[1:]

    def send(src, dst, ss, rs, to):
        return pltpu.make_async_remote_copy(
            src_ref=src, dst_ref=dst, send_sem=ss, recv_sem=rs, device_id=to, device_id_type=MESH
        )

    barrier = pltpu.get_barrier_semaphore()
    for peer in peers:
        pl.semaphore_signal(barrier, inc=1, device_id=peer, device_id_type=MESH)
    pl.semaphore_wait(barrier, len(peers))

    c_send = send(c_ref, cb.at[pl.ds(TOK, TOK)], x_ss.at[32], x_rs.at[32], x_mate)
    c_send.start()

    def column(half, i):
        away, sub = message(i)
        return pl.multiple_of(half * (D // 2) + ((z + away + 8) % 8) * KW + sub * SUB, SUB)

    def x_send(i):
        return send(
            x_ref.at[:, pl.ds(column(1 - xl, i), SUB)], xb.at[i, pl.ds(TOK, TOK)], x_ss.at[i], x_rs.at[i], x_mate
        )

    def x_load(i):
        return pltpu.make_async_copy(
            x_ref.at[:, pl.ds(column(xl, i), SUB)], xb.at[i, pl.ds(0, TOK)], x_ls.at[i]
        )

    w_src = w_ref.at[pl.ds(pl.multiple_of(piece * 64, 64), 64)]
    w_own = pltpu.make_async_copy(w_src, wg.at[xl, z, piece], l_s.at[0])
    c_own = pltpu.make_async_copy(c_ref, cb.at[pl.ds(0, TOK)], l_s.at[1])
    s_own = pltpu.make_async_copy(s_ref.at[0], sv, l_s.at[2])
    m_own = pltpu.make_async_copy(m_ref.at[0], mv, l_s.at[3])

    def ring(way, s):
        slot = wg.at[xl, (z + (8 - s if way == 0 else s)) % 8, piece]
        src = w_src if s == 0 else slot
        return send(src, slot, wa_ss.at[way, s], wa_rs.at[way, s], z_to[way])

    in_plane = (dev(y=y + 1), dev(y=y + 3), x_other)

    def plane(k, n):
        slot = wg.at[xl, (z + 8 - n) % 8, piece]
        return send(w_src if n == 0 else slot, slot, wb_ss.at[k, n], wb_rs.at[k, n], in_plane[k])

    def pass_on(way, s):
        ring(way, s).wait_recv()
        if s < (3 if way == 0 else 2):
            ring(way, s + 1).start()
        for k in range(3):
            plane(k, s + 1 if way == 0 else 7 - s).start()

    for i in range(2):
        x_send(i).start()
    ring(0, 0).start()
    ring(1, 0).start()
    for k in range(3):
        plane(k, 0).start()
    for i in range(2, 32):
        x_send(i).start()
    s_own.start()
    w_own.start()
    c_own.start()
    for i in range(32):
        x_load(i).start()
    m_own.start()
    pass_on(0, 0)
    pass_on(1, 0)

    s_own.wait()
    sel_row = lax.broadcasted_iota(jnp.int32, (KW // 2, KW), 0) // KEEP
    sel_col = lax.broadcasted_iota(jnp.int32, (KW // 2, KW), 1)
    spread = [
        jnp.where((sel_row == sel_col // BLOCK) & ((sel_col % BLOCK) // 16 == g), 1.0, 0.0).astype(bf16)
        for g in range(4)
    ]
    bit = lax.broadcasted_iota(jnp.int32, (SUB, KW), 1) % 16

    def mask_rows(b, carry):
        rows = pl.ds(pl.multiple_of(b * SUB, SUB), SUB)
        sel = sv[rows, :]
        power = jnp.left_shift(1, sel % 16).astype(f32)
        total = jnp.zeros((SUB, KW), f32)
        for g in range(4):
            total += dot(jnp.where(sel // 16 == g, power, 0.0).astype(bf16), spread[g])
        mk[rows, :] = (jnp.right_shift(total.astype(jnp.int32), bit) % 2).astype(f32)
        return carry

    lax.fori_loop(0, KW // SUB, mask_rows, 0)
    pass_on(0, 1)
    pass_on(1, 1)
    fwd_ref[0], fwd_ref[1] = split(cosine_tile(True))
    inv_ref[0], inv_ref[1] = split(cosine_tile(False))
    w_own.wait()
    c_own.wait()
    m_own.wait()

    def product(i):
        pltpu.make_async_copy(x_ref.at[:, pl.ds(0, SUB)], xb.at[i, pl.ds(0, TOK)], x_ls.at[i]).wait()
        send(xb.at[i, pl.ds(0, TOK)], xb.at[i, pl.ds(TOK, TOK)], x_ss.at[i], x_rs.at[i], x_mate).wait_recv()
        return lax.dot_general(xb[i], cb[...], (((0,), (0,)), ((), ())), preferred_element_type=f32)

    def z_copy(way, m):
        return send(zs.at[way, m], zr.at[way, m], z_ss.at[way, m], z_rs.at[way, m], z_to[way])

    def step(way, m, i, before):
        total = product(i)
        if before is not None:
            z_copy(way, before).wait_recv()
            total += zr[way, before].astype(f32)
        zs[way, m] = total.astype(bf16)
        z_copy(way, m).start()

    def steps(m):
        first, *before = SUMS[m]
        for way in range(2):
            step(way, m, first + way, before[way])

    def group(x_side, y_side, core):
        return wg.at[x_side, :, (y_side % 4) * 2 + core]

    def later(n, at, to):
        return send(at, at, wd_ss.at[n], wd_rs.at[n], to)

    def half_group(x_side, y_side, h):
        return wg.at[x_side, pl.ds(4 * h, 4), (y_side % 4) * 2 + c]

    wd = [
        later(0, group(xl, y, c), dev(y=y + 2)),
        later(1, group(1 - xl, y, c), dev(y=y + 3)),
        later(2, half_group(xl, y + 3, 0), x_other),
        later(3, half_group(xl, y + 3, 1), x_other),
        later(4, half_group(1 - xl, y + 3, 0), dev(y=y + 1)),
        later(5, half_group(1 - xl, y + 3, 1), dev(y=y + 1)),
    ]
    groups = [(xl, y), (xl, y + 3), (xl, y + 1), (1 - xl, y), (xl, y + 2), (1 - xl, y + 3), (1 - xl, y + 1), (1 - xl, y + 2)]
    wc = [
        send(group(*g, c), group(*g, c), wc_ss.at[k], wc_rs.at[k], core_mate) for k, g in enumerate(groups)
    ]

    def input_grad(k):
        half, place = groups[k]
        place = place % 4
        wc[k].wait_recv()

        for first in range(0, 8, 4):
            rows = wg[half, pl.ds(first, 4), pl.ds(place * 2, 2)].reshape(4 * SUB, KW)
            grads = lax.dot_general(
                cb[0:TOK], rows, (((1,), (1,)), ((), ())), preferred_element_type=f32
            ).astype(bf16)
            for n in range(4):
                col = pl.multiple_of(half * (D // 2) + (first + n) * KW + place * SUB, SUB)
                ig_ref[:, pl.ds(col, SUB)] = grads[:, n * SUB : (n + 1) * SUB]

    mine = pl.ds(pl.multiple_of(c * TILE, TILE), TILE)
    theirs = pl.ds(pl.multiple_of((1 - c) * TILE, TILE), TILE)
    span = [pl.ds(first * SUB, count * SUB) for first, count in ROUNDS]

    def piece_of(q, j):
        first, count = ROUNDS[q]
        return pl.ds(pl.multiple_of(first * SUB + j * (count * SUB // 8), 16), count * SUB // 8)

    own_piece = [piece_of(q, chip) for q in range(N_ROUNDS)]
    closing = {first + count - 1: q for q, (first, count) in enumerate(ROUNDS)}

    def pair(q):
        return send(out.at[span[q], theirs], cx.at[span[q]], p_ss.at[q], p_rs.at[q], core_mate)

    def pieces(q, k):
        to = ((xh + k // 4) % 2) * 4 + (y + k) % 4
        return send(pr.at[piece_of(q, to)], rb.at[own_piece[q]], g_ss.at[q, k - 1], g_rs.at[q, k - 1], chips[k])

    def shares(q, k):
        at = sb.at[own_piece[q], mine]
        return send(at, at, h_ss.at[q, k - 1], h_rs.at[q, k - 1], chips[k])

    def halves(q):
        at = sb.at[span[q], mine]
        return send(at, at, q_ss.at[q], q_rs.at[q], core_mate)

    def finish(b):
        rows = pl.ds(b * SUB, SUB)
        total = product(OWN[b]) + DECAY * mv[rows, :]
        z_copy(0, 10 + b).wait_recv()
        z_copy(1, 10 + b).wait_recv()
        total += zr[0, 10 + b].astype(f32) + zr[1, 10 + b].astype(f32)
        retained = mk[rows, :] * transform(total, fwd_ref)
        out[rows, :] = retained.astype(bf16)
        if b in closing:
            pair(closing[b]).start()
        nm_ref[rows, :] = total
        mk[rows, :] = retained

    def renew(b):
        rows = pl.ds(b * SUB, SUB)
        nm_ref[rows, :] -= transform(mk[rows, :], inv_ref)

    def scatter(q):
        pair(q).wait_recv()
        both = out[span[q], mine].astype(f32) + cx[span[q], :].astype(f32)
        pr[span[q], :] = both.astype(bf16)
        for k in FAR:
            pieces(q, k).start()

    def gather(q):
        rb[own_piece[q], :] = pr[own_piece[q], :]
        for k in range(1, 8):
            pieces(q, k).wait_recv()
        sb[own_piece[q], mine] = jnp.sum(rb[span[q], :].astype(f32).reshape(8, -1, TILE), axis=0).astype(bf16)
        for k in FAR:
            shares(q, k).start()

    def exchange(q):
        for k in range(1, 8):
            shares(q, k).wait_recv()
        halves(q).start()

    def result(q):
        halves(q).wait_recv()
        both = sb[span[q], :]
        for j in range(KW // TILE):
            cols = slice(j * TILE, (j + 1) * TILE)
            u_ref[span[q], cols] = (dot(both[:, cols], inv_ref[0]) + dot(both[:, cols], inv_ref[1])) * (1.0 / 16.0)

    c_send.wait_recv()
    steps(0)
    pass_on(0, 2)
    pass_on(1, 2)
    steps(1)
    steps(2)
    pass_on(0, 3)
    wd[0].start()
    wc[0].start()
    steps(3)
    input_grad(0)
    steps(4)
    for k in range(3):
        for n in range(8):
            plane(k, n).wait_recv()
    for k in (2, 3, 1):
        wd[k].start()
    for k in (3, 1, 2):
        wc[k].start()
    steps(5)
    input_grad(3)
    steps(6)
    input_grad(1)
    steps(7)
    wd[2].wait_recv()
    wd[4].start()
    steps(8)
    input_grad(2)
    steps(9)
    wd[3].wait_recv()
    wd[5].start()
    wc[5].start()
    wd[0].wait_recv()
    wc[4].start()
    steps(10)
    input_grad(5)
    steps(11)
    input_grad(4)
    steps(12)
    steps(13)
    wd[1].wait_recv()
    wc[6].start()
    finish(0)
    finish(1)
    finish(2)
    scatter(0)
    finish(3)
    scatter(1)
    scatter(2)
    wd[4].wait_recv()
    wd[5].wait_recv()
    wc[7].start()
    gather(0)
    c_send.wait_send()
    for i in range(32):
        x_send(i).wait_send()
    for s in range(4):
        ring(0, s).wait_send()
    for s in range(3):
        ring(1, s).wait_send()
    for k in range(3):
        for n in range(8):
            plane(k, n).wait_send()
    input_grad(6)
    renew(0)
    gather(1)
    renew(1)
    gather(2)
    renew(2)

    def drain(m, carry):
        z_copy(0, m).wait_send()
        z_copy(1, m).wait_send()
        return carry

    lax.fori_loop(0, 14, drain, 0)
    for copy in wd:
        copy.wait_send()
    exchange(0)
    input_grad(7)
    renew(3)
    for copy in wc:
        copy.wait_send()
    for q in range(N_ROUNDS):
        pair(q).wait_send()
        for k in range(1, 8):
            pieces(q, k).wait_send()
    exchange(1)
    result(0)
    for k in range(1, 8):
        shares(0, k).wait_send()
    for k in range(1, 8):
        shares(1, k).wait_send()
    exchange(2)
    result(1)
    for k in range(1, 8):
        shares(2, k).wait_send()
    result(2)
    for q in range(N_ROUNDS):
        halves(q).wait_send()


def flush(ig_ref, nm_ref, u_ref, ig_out, nm_out, u_out, sems):
    copies = [
        pltpu.make_async_copy(ig_ref.at[pl.ds(k * 64, 64)], ig_out.at[pl.ds(k * 64, 64)], sems.at[k]) for k in range(4)
    ]
    copies += [pltpu.make_async_copy(nm_ref, nm_out.at[0], sems.at[4]), pltpu.make_async_copy(u_ref, u_out, sems.at[5])]
    for copy in copies:
        copy.start()
    for copy in copies:
        copy.wait()


def local(activations, cotangent, key_weight, momentum, selection):
    hbm, vmem = pl.BlockSpec(memory_space=pltpu.HBM), pl.BlockSpec(memory_space=pltpu.VMEM)
    dma = pltpu.SemaphoreType.DMA
    outs = pl.pallas_call(
        kernel,
        out_shape=(
            jax.ShapeDtypeStruct((TOK, D), bf16),
            jax.ShapeDtypeStruct((KW, KW), f32),
            jax.ShapeDtypeStruct((KW, KW), f32),
        ),
        in_specs=[hbm] * 5,
        out_specs=(vmem, vmem, vmem),
        scratch_shapes=[
            pltpu.VMEM((32, 2 * TOK, SUB), bf16),
            pltpu.VMEM((2 * TOK, KW), bf16),
            pltpu.VMEM((2, 14, SUB, KW), bf16),
            pltpu.VMEM((2, 14, SUB, KW), bf16),
            pltpu.VMEM((2, 8, 8, 64, KW), bf16),
            pltpu.VMEM((KW, KW), f32),
            pltpu.VMEM((KW, KW // 2), jnp.int32),
            pltpu.VMEM((KW, KW), f32),
            pltpu.VMEM((KW, KW), bf16),
            pltpu.VMEM((KW, TILE), bf16),
            pltpu.VMEM((KW, TILE), bf16),
            pltpu.VMEM((KW, TILE), bf16),
            pltpu.VMEM((KW, KW), bf16),
            pltpu.VMEM((2, TILE, TILE), bf16),
            pltpu.VMEM((2, TILE, TILE), bf16),
            dma((33,)), dma((33,)), dma((32,)),
            dma((2, 14)), dma((2, 14)),
            dma((2, 4)), dma((2, 4)), dma((3, 8)), dma((3, 8)), dma((6,)), dma((6,)), dma((8,)), dma((8,)),
            dma((N_ROUNDS,)), dma((N_ROUNDS,)),
            dma((N_ROUNDS, 7)), dma((N_ROUNDS, 7)), dma((N_ROUNDS, 7)), dma((N_ROUNDS, 7)),
            dma((N_ROUNDS,)), dma((N_ROUNDS,)), dma((4,)),
        ],
        compiler_params=pltpu.CompilerParams(
            collective_id=0, has_side_effects=True, vmem_limit_bytes=VMEM_LIMIT
        ),
        name="demo_step",
    )(*(pltpu.with_memory_space_constraint(a, pltpu.HBM) for a in (activations, cotangent, key_weight, momentum, selection)))
    return pl.pallas_call(
        flush,
        out_shape=(
            jax.ShapeDtypeStruct((TOK, D), bf16),
            jax.ShapeDtypeStruct((1, KW, KW), f32),
            jax.ShapeDtypeStruct((KW, KW), f32),
        ),
        in_specs=[vmem] * 3,
        out_specs=(hbm, hbm, hbm),
        scratch_shapes=[dma((6,))],
        compiler_params=pltpu.CompilerParams(vmem_limit_bytes=FLUSH_LIMIT),
        name="flush",
    )(*outs)


def solution(mesh):
    in_specs = (
        P(("rep", "fsdp"), None),
        P(("rep", "fsdp"), None),
        P("fsdp", None),
        P("rep", "fsdp", None),
        P("rep", "fsdp", None),
    )
    out_specs = (P(("rep", "fsdp"), None), P("rep", "fsdp", None), P("fsdp", None))
    return jax.shard_map(local, mesh=mesh, in_specs=in_specs, out_specs=out_specs, check_vma=False)
```

```python
import functools

import jax
import jax.numpy as jnp
import numpy as np
from jax import lax
from jax.experimental import pallas as pl
from jax.experimental.pallas import tpu as pltpu
from jax.sharding import PartitionSpec as P

BLOCK = 64
KEEP = 32
DECAY = 0.9
MESH = pl.DeviceIdType.MESH
TOK = 256
D = 8192
KW = 512
SUB = 128
TILE = 256
ROUNDS = ((0, 2), (2, 1), (3, 1))
N_ROUNDS = len(ROUNDS)
VMEM_LIMIT = 44 << 20
FLUSH_LIMIT = 1 << 20
f32, bf16 = jnp.float32, jnp.bfloat16


def cosine_tile(flip):
    row = lax.broadcasted_iota(jnp.int32, (TILE, TILE), 1 if flip else 0)
    col = lax.broadcasted_iota(jnp.int32, (TILE, TILE), 0 if flip else 1)
    freq, where_at = row % BLOCK, col % BLOCK
    angle = ((2 * where_at + 1) * freq) % (4 * BLOCK)
    base = (2.0 / BLOCK) ** 0.5 * jnp.cos(angle.astype(f32) * (np.pi / (2 * BLOCK)))
    base = jnp.where(freq == 0, base * 0.5**0.5, base)
    return jnp.where(row // BLOCK == col // BLOCK, base, 0.0)


def split(a):
    hi = a.astype(bf16)
    return hi, (a - hi.astype(f32)).astype(bf16)


def dot(a, b):
    return jnp.dot(a, b, preferred_element_type=f32)


def transform(a, table):
    hi, lo = split(a)
    t_hi, t_lo = table[0], table[1]
    parts = []
    for j in range(a.shape[1] // TILE):
        cols = slice(j * TILE, (j + 1) * TILE)
        parts.append(dot(hi[:, cols], t_hi) + (dot(lo[:, cols], t_hi) + dot(hi[:, cols], t_lo)))
    return parts[0] if len(parts) == 1 else jnp.concatenate(parts, axis=1)


def message(i):
    if i < 4:
        return 4, i // 2 + 2 * (i % 2)
    if i < 20:
        sign, stage, slot = 1 - 2 * (i % 2), (i - 4) // 8, ((i - 4) % 8) // 2
        if stage == 0 and sign > 0:
            slot = (slot + 2) % 4
        return sign * (3 - stage), slot
    return [(1, 0), (-1, 0), (1, 1), (-1, 1), (1, 2), (-1, 2), (1, 3), (-1, 3), (0, 0), (0, 1), (0, 2), (0, 3)][i - 20]


FAR = (6, 5, 7, 4, 2, 1, 3)
OWN = [next(i for i in range(32) if message(i) == (0, b)) for b in range(4)]
SUMS = [
    (0, None, None), (2, None, None), (4, None, None), (6, None, None), (8, 0, 0), (10, 1, 1), (12, 4, 2),
    (14, 5, 3), (16, 2, 4), (18, 3, 5), (20, 6, 6), (22, 7, 7), (24, 8, 8), (26, 9, 9),
]


def kernel(
    x_ref, c_ref, w_ref, m_ref, s_ref,
    ig_ref, nm_ref, u_ref,
    xb, cb, zs, zr, wg, mv, sv, mk, out, cx, pr, rb, sb, fwd_ref, inv_ref,
    x_ss, x_rs, x_ls, z_ss, z_rs, wa_ss, wa_rs, wb_ss, wb_rs, wd_ss, wd_rs, wc_ss, wc_rs,
    p_ss, p_rs, g_ss, g_rs, h_ss, h_rs, q_ss, q_rs, l_s,
):
    r, f = lax.axis_index("rep"), lax.axis_index("fsdp")
    xh, y, c, xl, z = r // 8, (r // 2) % 4, r % 2, f // 8, f % 8
    chip = xh * 4 + y
    piece = y * 2 + c

    def dev(xh=xh, y=y, c=c, xl=xl, z=z):
        return (xh * 8 + (y % 4) * 2 + c, xl * 8 + z % 8)

    x_mate = dev(xl=1 - xl)
    x_other = dev(xh=1 - xh, xl=1 - xl)
    core_mate = dev(c=1 - c)
    z_to = (dev(z=z + 1), dev(z=z + 7))
    chips = [dev(xh=(xh + k // 4) % 2, y=y + k % 4) for k in range(8)]
    peers = [x_mate, x_other, core_mate, *z_to] + chips[1:]

    def send(src, dst, ss, rs, to):
        return pltpu.make_async_remote_copy(
            src_ref=src, dst_ref=dst, send_sem=ss, recv_sem=rs, device_id=to, device_id_type=MESH
        )

    barrier = pltpu.get_barrier_semaphore()
    for peer in peers:
        pl.semaphore_signal(barrier, inc=1, device_id=peer, device_id_type=MESH)
    pl.semaphore_wait(barrier, len(peers))

    c_send = send(c_ref, cb.at[pl.ds(TOK, TOK)], x_ss.at[1], x_rs.at[32], x_mate)
    c_send.start()

    def column(half, i):
        away, sub = message(i)
        return pl.multiple_of(half * (D // 2) + ((z + away + 8) % 8) * KW + sub * SUB, SUB)

    def x_send(i):
        return send(
            x_ref.at[:, pl.ds(column(1 - xl, i), SUB)], xb.at[i, pl.ds(TOK, TOK)], x_ss.at[0], x_rs.at[i], x_mate
        )

    def x_load(i):
        return pltpu.make_async_copy(
            x_ref.at[:, pl.ds(column(xl, i), SUB)], xb.at[i, pl.ds(0, TOK)], x_ls.at[i]
        )

    w_src = w_ref.at[pl.ds(pl.multiple_of(piece * 64, 64), 64)]
    w_own = pltpu.make_async_copy(w_src, wg.at[xl, z, piece], l_s.at[0])
    c_own = pltpu.make_async_copy(c_ref, cb.at[pl.ds(0, TOK)], l_s.at[1])
    s_own = pltpu.make_async_copy(s_ref.at[0], sv, l_s.at[2])
    m_own = pltpu.make_async_copy(m_ref.at[0], mv, l_s.at[3])

    def ring(way, s):
        slot = wg.at[xl, (z + (8 - s if way == 0 else s)) % 8, piece]
        src = w_src if s == 0 else slot
        return send(src, slot, wa_ss.at[way, s], wa_rs.at[way, s], z_to[way])

    in_plane = (dev(y=y + 1), dev(y=y + 3), x_other)

    def plane(k, n):
        slot = wg.at[xl, (z + 8 - n) % 8, piece]
        return send(w_src if n == 0 else slot, slot, wb_ss.at[k], wb_rs.at[k], in_plane[k])

    def pass_on(way, s):
        ring(way, s).wait_recv()
        if s < (3 if way == 0 else 2):
            ring(way, s + 1).start()
        for k in range(3):
            plane(k, s + 1 if way == 0 else 7 - s).start()

    for i in range(2):
        x_send(i).start()
    ring(0, 0).start()
    ring(1, 0).start()
    for k in range(3):
        plane(k, 0).start()
    for i in range(2, 32):
        x_send(i).start()
    s_own.start()
    w_own.start()
    c_own.start()
    for i in range(32):
        x_load(i).start()
    m_own.start()
    pass_on(0, 0)
    pass_on(1, 0)

    s_own.wait()
    sel_row = lax.broadcasted_iota(jnp.int32, (KW // 2, KW), 0) // KEEP
    sel_col = lax.broadcasted_iota(jnp.int32, (KW // 2, KW), 1)
    spread = [
        jnp.where((sel_row == sel_col // BLOCK) & ((sel_col % BLOCK) // 16 == g), 1.0, 0.0).astype(bf16)
        for g in range(4)
    ]
    bit = lax.broadcasted_iota(jnp.int32, (SUB, KW), 1) % 16

    def mask_rows(b, carry):
        rows = pl.ds(pl.multiple_of(b * SUB, SUB), SUB)
        sel = sv[rows, :]
        power = jnp.left_shift(1, sel % 16).astype(f32)
        total = jnp.zeros((SUB, KW), f32)
        for g in range(4):
            total += dot(jnp.where(sel // 16 == g, power, 0.0).astype(bf16), spread[g])
        mk[rows, :] = (jnp.right_shift(total.astype(jnp.int32), bit) % 2).astype(f32)
        return carry

    lax.fori_loop(0, KW // SUB, mask_rows, 0)
    pass_on(0, 1)
    pass_on(1, 1)
    fwd_ref[0], fwd_ref[1] = split(cosine_tile(True))
    inv_ref[0], inv_ref[1] = split(cosine_tile(False))
    w_own.wait()
    c_own.wait()
    m_own.wait()

    def product(i):
        pltpu.make_async_copy(x_ref.at[:, pl.ds(0, SUB)], xb.at[i, pl.ds(0, TOK)], x_ls.at[i]).wait()
        send(xb.at[i, pl.ds(0, TOK)], xb.at[i, pl.ds(TOK, TOK)], x_ss.at[0], x_rs.at[i], x_mate).wait_recv()
        return lax.dot_general(xb[i], cb[...], (((0,), (0,)), ((), ())), preferred_element_type=f32)

    def z_copy(way, m):
        return send(zs.at[way, m], zr.at[way, m], z_ss.at[0], z_rs.at[way, m], z_to[way])

    def step(way, m, i, before):
        total = product(i)
        if before is not None:
            z_copy(way, before).wait_recv()
            total += zr[way, before].astype(f32)
        zs[way, m] = total.astype(bf16)
        z_copy(way, m).start()

    def steps(m):
        first, *before = SUMS[m]
        for way in range(2):
            step(way, m, first + way, before[way])

    def group(x_side, y_side, core):
        return wg.at[x_side, :, (y_side % 4) * 2 + core]

    def later(n, at, to):
        return send(at, at, wd_ss.at[n], wd_rs.at[n], to)

    def half_group(x_side, y_side, h):
        return wg.at[x_side, pl.ds(4 * h, 4), (y_side % 4) * 2 + c]

    wd = [
        later(0, group(xl, y, c), dev(y=y + 2)),
        later(1, group(1 - xl, y, c), dev(y=y + 3)),
        later(2, half_group(xl, y + 3, 0), x_other),
        later(3, half_group(xl, y + 3, 1), x_other),
        later(4, half_group(1 - xl, y + 3, 0), dev(y=y + 1)),
        later(5, half_group(1 - xl, y + 3, 1), dev(y=y + 1)),
    ]
    groups = [(xl, y), (xl, y + 3), (xl, y + 1), (1 - xl, y), (xl, y + 2), (1 - xl, y + 3), (1 - xl, y + 1), (1 - xl, y + 2)]
    wc = [
        send(group(*g, c), group(*g, c), wc_ss.at[k], wc_rs.at[k], core_mate) for k, g in enumerate(groups)
    ]

    def input_grad(k):
        half, place = groups[k]
        place = place % 4
        wc[k].wait_recv()

        for first in range(0, 8, 4):
            rows = wg[half, pl.ds(first, 4), pl.ds(place * 2, 2)].reshape(4 * SUB, KW)
            grads = lax.dot_general(
                cb[0:TOK], rows, (((1,), (1,)), ((), ())), preferred_element_type=f32
            ).astype(bf16)
            for n in range(4):
                col = pl.multiple_of(half * (D // 2) + (first + n) * KW + place * SUB, SUB)
                ig_ref[:, pl.ds(col, SUB)] = grads[:, n * SUB : (n + 1) * SUB]

    mine = pl.ds(pl.multiple_of(c * TILE, TILE), TILE)
    theirs = pl.ds(pl.multiple_of((1 - c) * TILE, TILE), TILE)
    span = [pl.ds(first * SUB, count * SUB) for first, count in ROUNDS]

    def piece_of(q, j):
        first, count = ROUNDS[q]
        return pl.ds(pl.multiple_of(first * SUB + j * (count * SUB // 8), 16), count * SUB // 8)

    own_piece = [piece_of(q, chip) for q in range(N_ROUNDS)]
    closing = {first + count - 1: q for q, (first, count) in enumerate(ROUNDS)}

    def pair(q):
        return send(out.at[span[q], theirs], cx.at[span[q]], p_ss.at[q], p_rs.at[q], core_mate)

    def pieces(q, k):
        to = ((xh + k // 4) % 2) * 4 + (y + k) % 4
        return send(pr.at[piece_of(q, to)], rb.at[own_piece[q]], g_ss.at[q], g_rs.at[q], chips[k])

    def shares(q, k):
        at = sb.at[own_piece[q], mine]
        return send(at, at, h_ss.at[q], h_rs.at[q], chips[k])

    def seven(q, ss, rs):
        first, count = ROUNDS[q]
        at = pr.at[pl.ds(first * SUB, 7 * (count * SUB // 8))]
        return send(at, at, ss.at[q], rs.at[q], chips[1])

    def halves(q):
        at = sb.at[span[q], mine]
        return send(at, at, q_ss.at[q], q_rs.at[q], core_mate)

    def finish(b):
        rows = pl.ds(b * SUB, SUB)
        total = product(OWN[b]) + DECAY * mv[rows, :]
        z_copy(0, 10 + b).wait_recv()
        z_copy(1, 10 + b).wait_recv()
        total += zr[0, 10 + b].astype(f32) + zr[1, 10 + b].astype(f32)
        retained = mk[rows, :] * transform(total, fwd_ref)
        out[rows, :] = retained.astype(bf16)
        if b in closing:
            pair(closing[b]).start()
        nm_ref[rows, :] = total
        mk[rows, :] = retained

    def renew(b):
        rows = pl.ds(b * SUB, SUB)
        nm_ref[rows, :] -= transform(mk[rows, :], inv_ref)

    def scatter(q):
        pair(q).wait_recv()
        both = out[span[q], mine].astype(f32) + cx[span[q], :].astype(f32)
        pr[span[q], :] = both.astype(bf16)
        for k in FAR:
            pieces(q, k).start()

    def gather(q):
        rb[own_piece[q], :] = pr[own_piece[q], :]
        seven(q, g_ss, g_rs).wait_recv()
        sb[own_piece[q], mine] = jnp.sum(rb[span[q], :].astype(f32).reshape(8, -1, TILE), axis=0).astype(bf16)
        for k in FAR:
            shares(q, k).start()

    def exchange(q):
        seven(q, h_ss, h_rs).wait_recv()
        halves(q).start()

    def result(q):
        halves(q).wait_recv()
        both = sb[span[q], :]
        for j in range(KW // TILE):
            cols = slice(j * TILE, (j + 1) * TILE)
            u_ref[span[q], cols] = (dot(both[:, cols], inv_ref[0]) + dot(both[:, cols], inv_ref[1])) * (1.0 / 16.0)

    c_send.wait_recv()
    steps(0)
    pass_on(0, 2)
    pass_on(1, 2)
    steps(1)
    steps(2)
    pass_on(0, 3)
    wd[0].start()
    wc[0].start()
    steps(3)
    input_grad(0)
    steps(4)
    eight = [send(group(xl, y, c), group(xl, y, c), wb_ss.at[k], wb_rs.at[k], in_plane[k]) for k in range(3)]
    for copy in eight:
        copy.wait_recv()
    for k in (2, 3, 1):
        wd[k].start()
    for k in (3, 1, 2):
        wc[k].start()
    steps(5)
    input_grad(3)
    steps(6)
    input_grad(1)
    steps(7)
    wd[2].wait_recv()
    wd[4].start()
    steps(8)
    input_grad(2)
    steps(9)
    wd[3].wait_recv()
    wd[5].start()
    wc[5].start()
    wd[0].wait_recv()
    wc[4].start()
    steps(10)
    input_grad(5)
    steps(11)
    input_grad(4)
    steps(12)
    steps(13)
    wd[1].wait_recv()
    wc[6].start()
    finish(0)
    finish(1)
    finish(2)
    scatter(0)
    finish(3)
    scatter(1)
    scatter(2)
    wd[4].wait_recv()
    wd[5].wait_recv()
    wc[7].start()
    gather(0)
    c_send.wait_send()
    sent = xb.at[:, pl.ds(0, TOK)]
    send(sent, sent, x_ss.at[0], x_rs.at[0], x_mate).wait_send()
    for s in range(4):
        ring(0, s).wait_send()
    for s in range(3):
        ring(1, s).wait_send()
    for copy in eight:
        copy.wait_send()
    input_grad(6)
    renew(0)
    gather(1)
    renew(1)
    gather(2)
    renew(2)

    send(zs, zr, z_ss.at[0], z_rs.at[0, 0], z_to[0]).wait_send()
    for copy in wd:
        copy.wait_send()
    exchange(0)
    input_grad(7)
    renew(3)
    for copy in wc:
        copy.wait_send()
    for q in range(N_ROUNDS):
        pair(q).wait_send()
        seven(q, g_ss, g_rs).wait_send()
    exchange(1)
    result(0)
    seven(0, h_ss, h_rs).wait_send()
    seven(1, h_ss, h_rs).wait_send()
    exchange(2)
    result(1)
    seven(2, h_ss, h_rs).wait_send()
    result(2)
    for q in range(N_ROUNDS):
        halves(q).wait_send()


def flush(ig_ref, nm_ref, u_ref, ig_out, nm_out, u_out, sems):
    copies = [
        pltpu.make_async_copy(ig_ref.at[pl.ds(k * 64, 64)], ig_out.at[pl.ds(k * 64, 64)], sems.at[k]) for k in range(4)
    ]
    copies += [pltpu.make_async_copy(nm_ref, nm_out.at[0], sems.at[4]), pltpu.make_async_copy(u_ref, u_out, sems.at[5])]
    for copy in copies:
        copy.start()
    for copy in copies:
        copy.wait()


def local(activations, cotangent, key_weight, momentum, selection):
    hbm, vmem = pl.BlockSpec(memory_space=pltpu.HBM), pl.BlockSpec(memory_space=pltpu.VMEM)
    dma = pltpu.SemaphoreType.DMA
    outs = pl.pallas_call(
        kernel,
        out_shape=(
            jax.ShapeDtypeStruct((TOK, D), bf16),
            jax.ShapeDtypeStruct((KW, KW), f32),
            jax.ShapeDtypeStruct((KW, KW), f32),
        ),
        in_specs=[hbm] * 5,
        out_specs=(vmem, vmem, vmem),
        scratch_shapes=[
            pltpu.VMEM((32, 2 * TOK, SUB), bf16),
            pltpu.VMEM((2 * TOK, KW), bf16),
            pltpu.VMEM((2, 14, SUB, KW), bf16),
            pltpu.VMEM((2, 14, SUB, KW), bf16),
            pltpu.VMEM((2, 8, 8, 64, KW), bf16),
            pltpu.VMEM((KW, KW), f32),
            pltpu.VMEM((KW, KW // 2), jnp.int32),
            pltpu.VMEM((KW, KW), f32),
            pltpu.VMEM((KW, KW), bf16),
            pltpu.VMEM((KW, TILE), bf16),
            pltpu.VMEM((KW, TILE), bf16),
            pltpu.VMEM((KW, TILE), bf16),
            pltpu.VMEM((KW, KW), bf16),
            pltpu.VMEM((2, TILE, TILE), bf16),
            pltpu.VMEM((2, TILE, TILE), bf16),
            dma((2,)), dma((33,)), dma((32,)),
            dma((1,)), dma((2, 14)),
            dma((2, 4)), dma((2, 4)), dma((3,)), dma((3,)), dma((6,)), dma((6,)), dma((8,)), dma((8,)),
            dma((N_ROUNDS,)), dma((N_ROUNDS,)),
            dma((N_ROUNDS,)), dma((N_ROUNDS,)), dma((N_ROUNDS,)), dma((N_ROUNDS,)),
            dma((N_ROUNDS,)), dma((N_ROUNDS,)), dma((4,)),
        ],
        compiler_params=pltpu.CompilerParams(
            collective_id=0, has_side_effects=True, vmem_limit_bytes=VMEM_LIMIT
        ),
        name="demo_step",
    )(*(pltpu.with_memory_space_constraint(a, pltpu.HBM) for a in (activations, cotangent, key_weight, momentum, selection)))
    return pl.pallas_call(
        flush,
        out_shape=(
            jax.ShapeDtypeStruct((TOK, D), bf16),
            jax.ShapeDtypeStruct((1, KW, KW), f32),
            jax.ShapeDtypeStruct((KW, KW), f32),
        ),
        in_specs=[vmem] * 3,
        out_specs=(hbm, hbm, hbm),
        scratch_shapes=[dma((6,))],
        compiler_params=pltpu.CompilerParams(vmem_limit_bytes=FLUSH_LIMIT),
        name="flush",
    )(*outs)


def solution(mesh):
    in_specs = (
        P(("rep", "fsdp"), None),
        P(("rep", "fsdp"), None),
        P("fsdp", None),
        P("rep", "fsdp", None),
        P("rep", "fsdp", None),
    )
    out_specs = (P(("rep", "fsdp"), None), P("rep", "fsdp", None), P("fsdp", None))
    return jax.shard_map(local, mesh=mesh, in_specs=in_specs, out_specs=out_specs, check_vma=False)
```
